32 devices in a mesh: dom: 16 (over z, y, core), hid: 2 (over x).
Axes of the slice: x: 2, y: 2, z: 4, core: 2. Of those that a mesh axis runs over, the one named last changes fastest.
Arguments:
- features: bfloat16 [512, 16384], P(None, 'dom'), may hold values from -6 to 6
- weight: bfloat16 [512, 512], P(None, 'hid'), may hold values from -0.25 to 0.25
- band_tiles: bfloat16 [3072, 16384], P(None, 'dom'), may hold values from -0.109375 to 0.109375
- tile_live: int32 [12, 64], P(None, 'dom'), may hold values 0 or 1
- send_rows: int32 [16, 16, 128], P('dom'), may hold values from 0 to 1023
- recv_rows: int32 [16, 16, 128], P('dom'), may hold values from 0 to 1023
- edge_weight: float32 [16, 16, 128], P('dom'), may hold values from 0.25 to 1
- live_slots: int32 [16, 16], P('dom'), may hold values from 96 to 128, as said below
- bias_terms: float32 [512], P('hid'), may hold values from -3 to 3
- cotangent: bfloat16 [512, 16384], P('hid', 'dom'), may hold values from -6 to 6
Outputs:
- output: bfloat16 [512, 16384], P('hid', 'dom')
- feature_grad: bfloat16 [512, 16384], P('hid', 'dom')
- weight_grad: float32 [512, 512], P(None, 'hid')
- bias_grad: float32 [512], P('hid')
The draws below stay inside these ranges and needn't reach their ends.
Inputs may be any that keep to these rules, and one draw needn't show every extreme that they name: `live_slots`: every reader block has at least one owner block whose list has all 128 slots live.
All inputs are finite; a program needn't handle non-finite values. No bound on the sum of `tile_live` on one device may be relied on, other than what follows from the above.
Results may differ from the reference program's by a relative error of at most 0.0065.
Values may be sent and summed in bfloat16 or wider, within the bound.
No kernel may reach another device: no remote copies, remote signals or barrier semaphores. Data moves between devices by JAX's collectives and lax.ppermute only.
A program may use at most 64 MiB of HBM per device.

```python
import math
import jax
import jax.numpy as jnp
from jax import lax

F = 512
H = 512
TILE = 256
C = 128
R_DEV = 1024
N = 16384
PEERS = 16
N_DOM = 16


def draw_live_slots(key, part):
    base = jax.random.randint(jax.random.fold_in(key, 11), (PEERS, PEERS), 3 * C // 4, C + 1)
    full_at = jax.random.randint(jax.random.fold_in(key, 12), (PEERS,), 0, PEERS)
    column = jnp.arange(PEERS)[None, :]
    return jnp.where(column == full_at[:, None], C, base).astype(jnp.int32)


def with_ends(result, key, smallest, high):
    longest = result.shape.index(max(result.shape))
    spots = []
    for shift in (0, 1):
        where = [jax.random.randint(jax.random.fold_in(key, axis), (), 0, length) for axis, length in enumerate(result.shape)]
        where[longest] = (where[longest] + shift) % result.shape[longest]
        spots.append(tuple(where))
    return result.at[spots[0]].set(smallest).at[spots[1]].set(high)


def levels(rng, extent, pieces, low, high):
    def one(dim, parts):
        draws = jax.random.uniform(jax.random.fold_in(jax.random.fold_in(rng, 6), dim), (parts,), jnp.float32, low / len(pieces), high / len(pieces))
        return jnp.repeat(jnp.exp(draws), extent[dim] // parts).reshape((-1,) + (1,) * (len(extent) - dim - 1))

    factor_of = one(*pieces[0])
    for cut in pieces[1:]:
        factor_of = factor_of * one(*cut)
    return factor_of


def noise(key, dims, spread, bound, split=(), kind=jnp.bfloat16):
    values = spread * jax.random.normal(key, dims, jnp.float32)
    if split:
        values = values * levels(key, dims, split, -0.22, 0.18)
    return jnp.clip(values, -bound, bound).astype(kind)


def setup_inputs(seed: int = 0) -> dict:
    seeds = jax.random.split(jax.random.key(seed), 11)
    return {
        "features": noise(seeds[0], (F, N), 1.0, 6.0, ((1, 16),)),
        "weight": noise(seeds[1], (F, H), F ** -0.5, 0.25, ((1, 2),)),
        "band_tiles": noise(seeds[2], (3 * R_DEV, N), (3 * R_DEV) ** -0.5, 0.109375, ((1, 16),)),
        "tile_live": with_ends((jax.random.randint(seeds[3], (3 * R_DEV // TILE, N // TILE), 0, 4) < 3).astype(jnp.int32), jax.random.fold_in(seeds[3], 1), 0, 1),
        "send_rows": with_ends(jax.random.randint(seeds[4], (PEERS, PEERS, C), 0, R_DEV), jax.random.fold_in(seeds[4], 1), 0, R_DEV - 1).astype(jnp.int32),
        "recv_rows": with_ends(jax.random.randint(seeds[5], (PEERS, PEERS, C), 0, R_DEV), jax.random.fold_in(seeds[5], 1), 0, R_DEV - 1).astype(jnp.int32),
        "edge_weight": jnp.clip(jnp.exp(math.log(1.0) - 1.3862944 * jax.random.uniform(seeds[6], (PEERS, PEERS, C), jnp.float32) ** levels(seeds[6], (PEERS, PEERS, C), ((0, 16),), -0.2, 0.2)), 0.25, 1.0),
        "live_slots": draw_live_slots(jax.random.fold_in(seeds[10], 71), 0),
        "bias_terms": noise(seeds[8], (H,), 0.5, 3.0, ((0, 2),), jnp.float32),
        "cotangent": noise(seeds[9], (H, N), 1.0, 6.0, ((0, 2), (1, 16))),
    }


def silu_grad(value):
    gate = jax.nn.sigmoid(value)
    return gate * (1.0 + value * (1.0 - gate))

def reference(features, weight, band_tiles, tile_live, send_rows, recv_rows, edge_weight, live_slots, bias_terms, cotangent):
    part_count = N_DOM
    row_count = R_DEV
    mapped = jnp.dot(weight.T, features, preferred_element_type=jnp.float32).astype(jnp.bfloat16)
    tile_mask = tile_live.astype(jnp.bfloat16)
    dense = (band_tiles.reshape(3 * row_count // TILE, TILE, part_count * row_count // TILE, TILE) * tile_mask[:, None, :, None]).reshape(3 * row_count, part_count * row_count)
    dense_f = dense.astype(jnp.float32).reshape(3, row_count, part_count, row_count)
    mapped_f = mapped.astype(jnp.float32)
    blocks = mapped_f.reshape(H, part_count, row_count)
    dense_sum = jnp.zeros((H, part_count, row_count), jnp.float32)
    for offset in range(3):
        source = jnp.roll(blocks, -(offset - 1), axis=1)
        dense_sum = dense_sum + jnp.einsum('hdj,jdi->hdi', source, dense_f[offset])
    slot_ids = jnp.arange(C)[None, None, :]
    slot_weight = edge_weight * (slot_ids < live_slots[:, :, None]).astype(jnp.float32)
    pick_order = jnp.transpose(send_rows, (1, 0, 2))
    send_cols = (jnp.arange(part_count)[None, :, None] * row_count + pick_order).reshape(-1)
    recv_cols = (jnp.arange(part_count)[:, None, None] * row_count + recv_rows).reshape(-1)
    flat_weight = slot_weight.reshape(-1)
    values = mapped_f[:, send_cols] * flat_weight[None, :]
    sparse_sum = jnp.zeros((H, part_count * row_count), jnp.float32).at[:, recv_cols].add(values)
    act = dense_sum.reshape(H, part_count * row_count) + sparse_sum + bias_terms[:, None]
    output = jax.nn.silu(act).astype(jnp.bfloat16)
    pre_grad = (cotangent.astype(jnp.float32) * silu_grad(act)).astype(jnp.bfloat16)
    grad_f = pre_grad.astype(jnp.float32)
    grad_blocks = grad_f.reshape(H, part_count, row_count)
    map_grad = jnp.zeros((H, part_count, row_count), jnp.float32)
    for offset in range(3):
        term = jnp.einsum('hdi,jdi->hdj', grad_blocks, dense_f[offset])
        map_grad = map_grad + jnp.roll(term, offset - 1, axis=1)
    message = (grad_f[:, recv_cols] * flat_weight[None, :]).astype(jnp.bfloat16)
    map_grad = map_grad.reshape(H, part_count * row_count).at[:, send_cols].add(message.astype(jnp.float32))
    grad_b = map_grad.astype(jnp.bfloat16)
    weight_grad = jnp.dot(features, grad_b.T, preferred_element_type=jnp.float32)
    bias_grad = lax.optimization_barrier(jnp.sum(grad_f, axis=1))
    feature_grad = jnp.dot(weight, grad_b, preferred_element_type=jnp.float32).astype(jnp.bfloat16)
    return (output, feature_grad, weight_grad, bias_grad)
```

```python
import functools

import jax
import jax.numpy as jnp
from jax import lax
from jax.experimental import pallas as pl
from jax.experimental.pallas import tpu as pltpu
from jax.sharding import PartitionSpec as P

TILE = 256
F32 = jnp.float32
BF16 = jnp.bfloat16
VMEM = pl.BlockSpec(memory_space=pltpu.VMEM)
SMEM = pl.BlockSpec(memory_space=pltpu.SMEM)


def call(kernel, outs, operands, scalars=0, scratch=(), flops=0, mib=24):
    moved = sum(o.size * o.dtype.itemsize for o in (*operands, *outs))
    return pl.pallas_call(
        kernel,
        out_shape=tuple(outs),
        in_specs=[SMEM] * scalars + [VMEM] * (len(operands) - scalars),
        out_specs=tuple(VMEM for _ in outs),
        scratch_shapes=scratch,
        compiler_params=pltpu.CompilerParams(vmem_limit_bytes=mib * 1024 * 1024),
        cost_estimate=pl.CostEstimate(flops=flops, bytes_accessed=moved, transcendentals=0),
    )(*operands)


def out(shape, dtype):
    return jax.ShapeDtypeStruct(shape, dtype)


def shifted(block, axis, distance):
    size = lax.axis_size(axis)
    return lax.ppermute(block, axis, [((i + distance) % size, i) for i in range(size)])


def swapped(block, axis, bit):
    size = lax.axis_size(axis)
    return lax.ppermute(block, axis, [(i, i ^ bit) for i in range(size)])


def dot(a, b):
    return jnp.dot(a, b, preferred_element_type=F32)


def slots_by_nodes(hot, rows_t, nodes, first, count, weights_t=None):
    slots = rows_t.shape[0]
    lanes = lax.broadcasted_iota(jnp.int32, (slots, nodes), 1)
    for p in range(first, first + count):
        value = 1.0 if weights_t is None else weights_t[:, p : p + 1]
        hot[p * slots : (p + 1) * slots, :] = jnp.where(
            rows_t[:, p : p + 1] == lanes, value, 0.0
        ).astype(BF16)


def nodes_by_slots(hot, rows, nodes, weights=None):
    peers, slots = rows.shape
    lines = lax.broadcasted_iota(jnp.int32, (nodes, slots), 0)
    for p in range(peers):
        value = 1.0 if weights is None else weights[p : p + 1, :]
        hot[:, p * slots : (p + 1) * slots] = jnp.where(
            rows[p : p + 1, :] == lines, value, 0.0
        ).astype(BF16)


def gather_kernel(hid_ref, features_ref, send_ref, out_ref, hot):
    peers, slots, rows = out_ref.shape
    nodes = features_ref.shape[1]
    start = pl.multiple_of(hid_ref[0] * rows, rows)
    block_t = features_ref[pl.ds(start, rows), :].T
    send_t = send_ref[...].T
    group = 4
    for p in range(0, peers, group):
        slots_by_nodes(hot, send_t, nodes, p, group)
        picked = dot(hot[p * slots : (p + group) * slots, :], block_t)
        out_ref[p : p + group] = picked.astype(BF16).reshape(group, slots, rows)


def dense_forward_kernel(live_ref, tiles_ref, own_ref, before_ref, after_ref, out_ref, total):
    rows, nodes = own_ref.shape
    blocks = nodes // TILE
    total[...] = jnp.zeros_like(total)
    for s, ref in enumerate((before_ref, own_ref, after_ref)):
        for j in range(blocks):
            left = ref[:, j * TILE : (j + 1) * TILE]
            line = s * blocks + j
            for i in range(blocks):
                tile = tiles_ref[line * TILE : (line + 1) * TILE, i * TILE : (i + 1) * TILE]
                live = live_ref[line, i].astype(F32)
                total[:, i * TILE : (i + 1) * TILE] += dot(left, tile) * live
    out_ref[...] = total[...].T


def masked_weights(weight, counts):
    slots = lax.broadcasted_iota(jnp.int32, weight.shape, 1)
    return jnp.where(slots < counts, weight, 0.0)


def lists_kernel(send_ref, recv_ref, weight_ref, counts_ref, nodes_in_ref, slots_in_ref, nodes_out_ref):
    weights = masked_weights(weight_ref[...], counts_ref[...])
    nodes = slots_in_ref.shape[1]
    nodes_by_slots(nodes_in_ref, recv_ref[...], nodes, weights)
    slots_by_nodes(slots_in_ref, recv_ref[...].T, nodes, 0, recv_ref.shape[0], weights.T)
    nodes_by_slots(nodes_out_ref, send_ref[...], nodes)


def turn_kernel(*refs):
    out_ref = refs[-1]
    width = refs[0].shape[0]
    for k, ref in enumerate(refs[:-1]):
        out_ref[:, k * width : (k + 1) * width] = ref[...].T


def aggregate_kernel(arrived_ref, nodes_in_ref, dense_ref, out_ref):
    peers, slots, rows = arrived_ref.shape
    arrived = arrived_ref[...].reshape(peers * slots, rows)
    out_ref[...] = (dense_ref[...] + dot(nodes_in_ref[...], arrived)).astype(BF16)


def layer_kernel(n_hid, hid_ref, weight_ref, bias_ref, cotangent_ref, slots_in_ref, *refs):
    aggs, (output_ref, grad_ref, back_ref, message_ref) = refs[:n_hid], refs[n_hid:]
    rows = aggs[0].shape[1]
    width = output_ref.shape[1]
    act = jnp.broadcast_to(bias_ref[...], cotangent_ref.shape)
    for k, ref in enumerate(aggs):
        start = pl.multiple_of(lax.rem(hid_ref[0] + k, n_hid) * rows, rows)
        act = act + dot(ref[...], weight_ref[pl.ds(start, rows), :])
    gate = 1.0 / (1.0 + jnp.exp(-act))
    output_ref[...] = (act[:, :width] * gate[:, :width]).astype(BF16)
    slope = gate * (1.0 + act * (1.0 - gate))
    grad = (cotangent_ref[...].astype(F32) * slope).astype(BF16)
    grad_ref[...] = grad[:, :width]
    start = pl.multiple_of(hid_ref[0] * rows, rows)
    back = lax.dot_general(
        grad, weight_ref[pl.ds(start, rows), :], (((1,), (1,)), ((), ())), preferred_element_type=F32
    ).astype(BF16)
    back_ref[...] = back
    peers, slots, _ = message_ref.shape
    message_ref[...] = dot(slots_in_ref[...], back).astype(BF16).reshape(peers, slots, rows)


def dense_backward_kernel(parts, live_ref, tiles_ref, back_ref, *out_refs):
    nodes = back_ref.shape[0]
    blocks = nodes // TILE
    for s, out_ref in zip(parts, out_refs):
        for j in range(blocks):
            line = s * blocks + j
            total = None
            for i in range(blocks):
                tile = tiles_ref[line * TILE : (line + 1) * TILE, i * TILE : (i + 1) * TILE]
                live = live_ref[line, i].astype(F32)
                term = dot(tile, back_ref[i * TILE : (i + 1) * TILE, :]) * live
                total = term if total is None else total + term
            out_ref[j * TILE : (j + 1) * TILE, :] = total.astype(out_ref.dtype)


def weight_kernel(n_hid, hid_ref, output_ref, grad_ref, *refs):
    aggs, (turned_ref, part_ref) = refs[:n_hid], refs[n_hid:]
    rows = aggs[0].shape[1]
    grad = grad_ref[...]
    turned_ref[...] = output_ref[...].T
    for k, ref in enumerate(aggs):
        start = pl.multiple_of(lax.rem(hid_ref[0] + k, n_hid) * rows, rows)
        part_ref[pl.ds(start, rows), :] = dot(ref[...].T, grad)
    total = jnp.sum(grad.astype(F32), axis=0, keepdims=True)
    size = n_hid * rows
    part_ref[size:, :] = jnp.broadcast_to(total, (part_ref.shape[0] - size, part_ref.shape[1]))


def scatter_kernel(returned_ref, nodes_out_ref, own_ref, before_ref, after_ref, out_ref):
    peers, slots, rows = returned_ref.shape
    returned = returned_ref[...].reshape(peers * slots, rows)
    total = own_ref[...] + before_ref[...].astype(F32) + after_ref[...].astype(F32)
    total = total + dot(nodes_out_ref[...], returned)
    out_ref[...] = total.astype(BF16).T


def summed_over(part, axis):
    size = lax.axis_size(axis)
    half = part.shape[0] // 2
    odd = lax.rem(lax.axis_index(axis), 2) == 1
    low, high = part[:half], part[half:]
    arrived = swapped(jnp.where(odd, low, high).astype(BF16), axis, 1)
    mine = jnp.where(odd, high, low) + arrived.astype(F32)
    bit = 2
    while bit < size:
        sent = mine.astype(BF16)
        mine = sent.astype(F32) + swapped(sent, axis, bit).astype(F32)
        bit *= 2
    other = swapped(mine, axis, 1)
    return jnp.concatenate([jnp.where(odd, other, mine), jnp.where(odd, mine, other)])


def on_device(
    features,
    weight,
    band_tiles,
    tile_live,
    send_rows,
    recv_rows,
    edge_weight,
    live_slots,
    bias_terms,
    cotangent,
):
    n_hid = lax.axis_size("hid")
    hid = lax.axis_index("hid").astype(jnp.int32).reshape(1)
    peers, slots = send_rows.shape[1:]
    nodes = features.shape[1]
    width = weight.shape[1]
    rows = features.shape[0] // n_hid
    lists = peers * slots
    send, recv = send_rows[0], recv_rows[0]

    (outgoing,) = call(
        gather_kernel,
        [out((peers, slots, rows), BF16)],
        [hid, features, send],
        1,
        [pltpu.VMEM((lists, nodes), BF16)],
        flops=2 * lists * nodes * rows,
    )
    arrived = lax.all_to_all(outgoing, "dom", split_axis=0, concat_axis=0, tiled=True)

    own = lax.dynamic_slice_in_dim(features, hid[0] * rows, rows, 0)
    before, after = shifted(own, "dom", -1), shifted(own, "dom", 1)
    steps = range(1, n_hid)
    weights = jnp.concatenate([weight] + [shifted(weight, "hid", k) for k in steps], axis=1)
    biases = jnp.concatenate([bias_terms] + [shifted(bias_terms, "hid", k) for k in steps])
    cotangents = [cotangent] + [shifted(cotangent, "hid", k) for k in steps]

    (dense,) = call(
        dense_forward_kernel,
        [out((nodes, rows), F32)],
        [tile_live, band_tiles, own, before, after],
        1,
        [pltpu.VMEM((rows, nodes), F32)],
        flops=6 * nodes * nodes * rows,
    )
    nodes_in, slots_in, nodes_out = call(
        lists_kernel,
        [out((nodes, lists), BF16), out((lists, nodes), BF16), out((nodes, lists), BF16)],
        [send, recv, edge_weight[0], live_slots.reshape(peers, 1)],
        flops=2 * lists * nodes * rows,
        mib=40,
    )
    (cotangent_t,) = call(turn_kernel, [out((nodes, n_hid * width), BF16)], cotangents)

    (agg,) = call(
        aggregate_kernel,
        [out((nodes, rows), BF16)],
        [arrived, nodes_in, dense],
        flops=2 * lists * nodes * rows,
    )
    aggs = [agg] + [shifted(agg, "hid", k) for k in steps]
    output_t, grad, back, message = call(
        functools.partial(layer_kernel, n_hid),
        [out((nodes, width), BF16), out((nodes, width), BF16), out((nodes, rows), BF16), out((peers, slots, rows), BF16)],
        [hid, weights, biases[None, :], cotangent_t, slots_in, *aggs],
        1,
        flops=2 * lists * nodes * rows,
        mib=32,
    )
    returned = lax.all_to_all(message, "dom", split_axis=0, concat_axis=0, tiled=True)

    to_before, to_after = call(
        functools.partial(dense_backward_kernel, (0, 2)),
        [out((nodes, rows), BF16)] * 2,
        [tile_live, band_tiles, back],
        1,
        flops=4 * nodes * nodes * rows,
    )
    from_after, from_before = shifted(to_before, "dom", 1), shifted(to_after, "dom", -1)
    (kept,) = call(
        functools.partial(dense_backward_kernel, (1,)),
        [out((nodes, rows), F32)],
        [tile_live, band_tiles, back],
        1,
        flops=2 * nodes * nodes * rows,
    )
    pad = 32
    output, part = call(
        functools.partial(weight_kernel, n_hid),
        [out((width, nodes), BF16), out((n_hid * rows + pad, width), F32)],
        [hid, output_t, grad, *aggs],
        1,
        flops=2 * nodes * n_hid * rows * width,
    )
    total = summed_over(part, "dom")
    weight_grad, bias_grad = total[: n_hid * rows], total[n_hid * rows]
    (feature_grad,) = call(
        scatter_kernel,
        [out((rows, nodes), BF16)],
        [returned, nodes_out, kept, from_before, from_after],
        flops=2 * lists * nodes * rows,
    )
    return (output, feature_grad, weight_grad, bias_grad)


def solution(mesh):
    return jax.shard_map(
        on_device,
        mesh=mesh,
        in_specs=(
            P(None, "dom"),
            P(None, "hid"),
            P(None, "dom"),
            P(None, "dom"),
            P("dom", None, None),
            P("dom", None, None),
            P("dom", None, None),
            P("dom", None),
            P("hid"),
            P("hid", "dom"),
        ),
        out_specs=(P("hid", "dom"), P("hid", "dom"), P(None, "hid"), P("hid")),
        check_vma=False,
    )
```

```python
import functools

import jax
import jax.numpy as jnp
from jax import lax
from jax.experimental import pallas as pl
from jax.experimental.pallas import tpu as pltpu
from jax.sharding import PartitionSpec as P

TILE = 256
F32 = jnp.float32
BF16 = jnp.bfloat16
VMEM = pl.BlockSpec(memory_space=pltpu.VMEM)
SMEM = pl.BlockSpec(memory_space=pltpu.SMEM)
HBM = pl.BlockSpec(memory_space=pltpu.HBM)


def call(kernel, outs, operands, scratch=(), us=1, mib=16, place=VMEM):
    arrays = [array for _, array in operands]
    return pl.pallas_call(
        kernel,
        out_shape=tuple(outs),
        in_specs=[place for place, _ in operands],
        out_specs=tuple(place for _ in outs),
        scratch_shapes=scratch,
        compiler_params=pltpu.CompilerParams(vmem_limit_bytes=mib * 1024 * 1024),
        cost_estimate=pl.CostEstimate(flops=us * 1000**3, bytes_accessed=1, transcendentals=0),
    )(*arrays)


def out(shape, dtype):
    return jax.ShapeDtypeStruct(shape, dtype)


def shifted(block, axis, distance):
    size = lax.axis_size(axis)
    return lax.ppermute(block, axis, [((i + distance) % size, i) for i in range(size)])


def swapped(block, axis, bit):
    size = lax.axis_size(axis)
    return lax.ppermute(block, axis, [(i, i ^ bit) for i in range(size)])


def dot(a, b):
    return jnp.dot(a, b, preferred_element_type=F32)


def slots_by_nodes(hot, rows_t, nodes, first, count, weights_t=None):
    slots = rows_t.shape[0]
    lanes = lax.broadcasted_iota(jnp.int32, (slots, nodes), 1)
    for p in range(first, first + count):
        value = 1.0 if weights_t is None else weights_t[:, p : p + 1]
        hot[p * slots : (p + 1) * slots, :] = jnp.where(
            rows_t[:, p : p + 1] == lanes, value, 0.0
        ).astype(BF16)


def nodes_by_slots(hot, rows, nodes, weights=None):
    peers, slots = rows.shape
    lines = lax.broadcasted_iota(jnp.int32, (nodes, slots), 0)
    for p in range(peers):
        value = 1.0 if weights is None else weights[p : p + 1, :]
        hot[:, p * slots : (p + 1) * slots] = jnp.where(
            rows[p : p + 1, :] == lines, value, 0.0
        ).astype(BF16)


def masked_weights(weight, counts):
    slots = lax.broadcasted_iota(jnp.int32, weight.shape, 1)
    return jnp.where(slots < counts, weight, 0.0)


class Copies:
    def __init__(self, sems):
        self.sems, self.started = sems, []

    def start(self, source, target):
        copy = pltpu.make_async_copy(source, target, self.sems.at[len(self.started)])
        copy.start()
        self.started.append(copy)
        return copy


def vmem(shape, dtype):
    return pltpu.VMEM(shape, dtype)


def sems(count):
    return pltpu.SemaphoreType.DMA((count,))


def gather_kernel(hid_ref, features_ref, send_ref, out_ref, hot, block, lists, picked, sems):
    peers, slots, rows = out_ref.shape
    nodes = features_ref.shape[1]
    copies = Copies(sems)
    start = pl.multiple_of(hid_ref[0] * rows, rows)
    lists_copy = copies.start(send_ref, lists)
    block_copy = copies.start(features_ref.at[pl.ds(start, rows), :], block)
    lists_copy.wait()
    send_t = lists[...].T
    group = 4
    slots_by_nodes(hot, send_t, nodes, 0, group)
    block_copy.wait()
    sent = []
    block_t = block[...].T
    for p in range(0, peers, group):
        part = dot(hot[p * slots : (p + group) * slots, :], block_t)
        picked[p : p + group] = part.astype(BF16).reshape(group, slots, rows)
        sent.append(copies.start(picked.at[pl.ds(p, group)], out_ref.at[pl.ds(p, group)]))
        if p + group < peers:
            slots_by_nodes(hot, send_t, nodes, p + group, group)
    for copy in sent:
        copy.wait()


def live_lines(live_ref, s, i, side, axis):
    shape = (1, side * TILE) if axis else (side * TILE, 1)
    place = lax.broadcasted_iota(jnp.int32, shape, axis) // TILE
    live = jnp.zeros(shape, F32)
    for j in range(side):
        live = jnp.where(place == j, live_ref[s * side + j, i].astype(F32), live)
    return live.astype(BF16)


def dense_forward(live_ref, tiles_ref, block_ref, s, i, first):
    nodes = block_ref.shape[1]
    side = nodes // TILE
    left = block_ref[...] * live_lines(live_ref, s, i, side, 1)
    return dot(left, tiles_ref[first : first + nodes, i * TILE : (i + 1) * TILE])


def dense_kernel(live_ref, tiles_ref, before_ref, own_ref, after_ref, out_ref):
    nodes = out_ref.shape[0]
    for i in range(nodes // TILE):
        total = None
        for s, ref in enumerate((before_ref, own_ref, after_ref)):
            term = dense_forward(live_ref, tiles_ref, ref, s, i, s * nodes)
            total = term if total is None else total + term
        out_ref[i * TILE : (i + 1) * TILE, :] = total.T


def aggregate_kernel(recv_ref, weight_ref, counts_ref, arrived_ref, dense_ref, out_ref, hot):
    peers, slots, rows = arrived_ref.shape
    nodes_by_slots(hot, recv_ref[...], out_ref.shape[0], masked_weights(weight_ref[...], counts_ref[...]))
    arrived = arrived_ref[...].reshape(peers * slots, rows)
    out_ref[...] = (dense_ref[...] + dot(hot[...], arrived)).astype(BF16)


def dense_backward(live_ref, tiles, block, s, first):
    nodes = block.shape[0]
    side = nodes // TILE
    place = lax.broadcasted_iota(jnp.int32, (nodes, 1), 0) // TILE
    for j in range(side):
        live = jnp.zeros((nodes, 1), F32)
        for i in range(side):
            live = jnp.where(place == i, live_ref[s * side + j, i].astype(F32), live)
        row = first + j * TILE
        yield j, dot(tiles[row : row + TILE, :], block * live.astype(BF16))


def dense_backward_kernel(parts, live_ref, tiles_ref, back_ref, *out_refs):
    nodes = back_ref.shape[0]
    for s, out_ref in zip(parts, out_refs):
        for j, term in dense_backward(live_ref, tiles_ref, back_ref[...], s, s * nodes):
            out_ref[j * TILE : (j + 1) * TILE, :] = term.astype(out_ref.dtype)


def weight_parts(hid_ref, grad, aggs, part_ref):
    n_hid, _, rows = aggs.shape
    for k in range(n_hid):
        start = pl.multiple_of(lax.rem(hid_ref[0] + k, n_hid) * rows, rows)
        part_ref[pl.ds(start, rows), :] = dot(aggs[k].T, grad)
    total = jnp.sum(grad.astype(F32), axis=0, keepdims=True)
    size = n_hid * rows
    part_ref[size:, :] = jnp.broadcast_to(total, (part_ref.shape[0] - size, part_ref.shape[1]))


def layer_kernel(n_hid, hid_ref, *refs):
    take = iter(refs)
    weights, biases, cotangents = ([next(take) for _ in range(n_hid)] for _ in range(3))
    aggs, recv_ref, weight_ref, counts_ref, output_ref, part_ref, back_ref, message_ref, hot = take
    peers, slots, rows = message_ref.shape
    width, nodes = output_ref.shape
    own = pl.ds(pl.multiple_of(hid_ref[0] * rows, rows), rows)
    total = None
    for k in range(n_hid):
        act = jnp.broadcast_to(biases[k][...], (nodes, width))
        for j in range(n_hid):
            start = pl.multiple_of(lax.rem(hid_ref[0] + j, n_hid) * rows, rows)
            act = act + dot(aggs[j], weights[k][pl.ds(start, rows), :])
        gate = 1.0 / (1.0 + jnp.exp(-act))
        slope = gate * (1.0 + act * (1.0 - gate))
        grad = (cotangents[k][...].T.astype(F32) * slope).astype(BF16)
        if k == 0:
            output_ref[...] = (act * gate).astype(BF16).T
            weight_parts(hid_ref, grad, aggs, part_ref)
        term = lax.dot_general(
            grad, weights[k][own, :], (((1,), (1,)), ((), ())), preferred_element_type=F32
        )
        total = term if total is None else total + term
    back = total.astype(BF16)
    back_ref[...] = back
    weights_t = masked_weights(weight_ref[...], counts_ref[...]).T
    recv_t = recv_ref[...].T
    group = 4
    for p in range(0, peers, group):
        slots_by_nodes(hot, recv_t, nodes, p, group, weights_t)
        picked = dot(hot[p * slots : (p + group) * slots, :], back)
        message_ref[p : p + group] = picked.astype(BF16).reshape(group, slots, rows)


def joined_kernel(odd_ref, mine_ref, other_ref, weight_ref, bias_ref):
    half = mine_ref.shape[0]
    odd = odd_ref[0] == 1
    low = jnp.where(odd, other_ref[...], mine_ref[...])
    high = jnp.where(odd, mine_ref[...], other_ref[...])
    size = weight_ref.shape[0]
    weight_ref[:half, :] = low
    weight_ref[half:, :] = high[: size - half, :]
    bias_ref[...] = high[size - half : size - half + 1, :]


def scatter_kernel(send_ref, returned_ref, own_ref, before_ref, after_ref, out_ref, hot):
    peers, slots, rows = returned_ref.shape
    nodes_by_slots(hot, send_ref[...], own_ref.shape[0])
    returned = returned_ref[...].reshape(peers * slots, rows)
    total = own_ref[...] + before_ref[...].astype(F32) + after_ref[...].astype(F32)
    total = total + dot(hot[...], returned)
    out_ref[...] = total.astype(BF16).T


def halved(part, axis, bits):
    place = lax.axis_index(axis)
    for bit in bits:
        odd = lax.rem(place // bit, 2) == 1
        half = part.shape[0] // 2
        low, high = part[:half], part[half:]
        arrived = swapped(jnp.where(odd, low, high).astype(BF16), axis, bit)
        part = jnp.where(odd, high, low) + arrived.astype(F32)
    return part


def doubled(part, axis, bits):
    for bit in bits:
        sent = part.astype(BF16)
        part = sent.astype(F32) + swapped(sent, axis, bit).astype(F32)
    return part


def joined(part, axis, bits):
    place = lax.axis_index(axis)
    for bit in reversed(bits):
        odd = lax.rem(place // bit, 2) == 1
        other = swapped(part, axis, bit)
        part = jnp.concatenate([jnp.where(odd, other, part), jnp.where(odd, part, other)])
    return part


def on_device(
    features,
    weight,
    band_tiles,
    tile_live,
    send_rows,
    recv_rows,
    edge_weight,
    live_slots,
    bias_terms,
    cotangent,
):
    n_hid = lax.axis_size("hid")
    hid = (SMEM, lax.axis_index("hid").astype(jnp.int32).reshape(1))
    peers, slots = send_rows.shape[1:]
    nodes = features.shape[1]
    width = weight.shape[1]
    rows = features.shape[0] // n_hid
    lists = peers * slots
    send, recv = (VMEM, send_rows[0]), (VMEM, recv_rows[0])
    edges = [recv, (VMEM, edge_weight[0]), (VMEM, live_slots.reshape(peers, 1))]
    tiles = [(SMEM, tile_live), (VMEM, band_tiles)]
    steps = range(1, n_hid)

    own = lax.dynamic_slice_in_dim(features, hid[1][0] * rows, rows, 0)
    before, after = shifted(own, "dom", -1), shifted(own, "dom", 1)
    (outgoing,) = call(
        gather_kernel,
        [out((peers, slots, rows), BF16)],
        [hid, (HBM, features), (HBM, send_rows[0])],
        [
            vmem((lists, nodes), BF16),
            vmem((rows, nodes), BF16),
            vmem((peers, slots), jnp.int32),
            vmem((peers, slots, rows), BF16),
            sems(peers + 2),
        ],
        mib=58,
        place=HBM,
    )
    arrived = lax.all_to_all(outgoing, "dom", split_axis=0, concat_axis=0, tiled=True)

    before, weight, bias_terms, cotangent = lax.optimization_barrier(
        (before, weight, bias_terms, cotangent)
    )
    weights = [weight] + [shifted(weight, "hid", k) for k in steps]
    biases = [bias_terms] + [shifted(bias_terms, "hid", k) for k in steps]
    cotangents = [cotangent] + [shifted(cotangent, "hid", k) for k in steps]
    (dense,) = call(
        dense_kernel,
        [out((nodes, rows), F32)],
        [*tiles, (VMEM, before), (VMEM, own), (VMEM, after)],
        us=60,
    )
    dense, weights, biases, cotangents = lax.optimization_barrier((dense, weights, biases, cotangents))
    (agg,) = call(
        aggregate_kernel,
        [out((nodes, rows), BF16)],
        [*edges, (VMEM, arrived), (VMEM, dense)],
        [vmem((nodes, lists), BF16)],
        us=4,
    )
    aggs = jnp.stack([agg] + [shifted(agg, "hid", k) for k in steps])
    pad = 64
    output, part, back, message = call(
        functools.partial(layer_kernel, n_hid),
        [
            out((width, nodes), BF16),
            out((n_hid * rows + pad, width), F32),
            out((nodes, rows), BF16),
            out((peers, slots, rows), BF16),
        ],
        [
            hid,
            *[(VMEM, w) for w in weights],
            *[(VMEM, b[None, :]) for b in biases],
            *[(VMEM, c) for c in cotangents],
            (VMEM, aggs),
            *edges,
        ],
        [vmem((lists, nodes), BF16)],
        us=6,
        mib=24,
    )
    returned = lax.all_to_all(message, "dom", split_axis=0, concat_axis=0, tiled=True)

    to_before, to_after = call(
        functools.partial(dense_backward_kernel, (0, 2)),
        [out((nodes, rows), BF16)] * 2,
        [*tiles, (VMEM, back)],
    )
    (kept,) = call(
        functools.partial(dense_backward_kernel, (1,)),
        [out((nodes, rows), F32)],
        [*tiles, (VMEM, back)],
    )
    bits = [1 << b for b in range((peers - 1).bit_length())]
    part = halved(part, "dom", bits[:1])
    part, to_before, to_after = lax.optimization_barrier((part, to_before, to_after))
    from_after, from_before = shifted(to_before, "dom", 1), shifted(to_after, "dom", -1)
    part = halved(part, "dom", bits[1:2])
    part = doubled(part, "dom", bits[2:3])
    part, from_after, from_before, kept = lax.optimization_barrier((part, from_after, from_before, kept))
    part = doubled(part, "dom", bits[3:])
    (feature_grad,) = call(
        scatter_kernel,
        [out((rows, nodes), BF16)],
        [send, (VMEM, returned), (VMEM, kept), (VMEM, from_before), (VMEM, from_after)],
        [vmem((nodes, lists), BF16)],
    )
    part = joined(part, "dom", bits[1:2])
    part, feature_grad = lax.optimization_barrier((part, feature_grad))
    odd = lax.rem(lax.axis_index("dom"), 2).astype(jnp.int32).reshape(1)
    weight_grad, bias_grad = call(
        joined_kernel,
        [out((n_hid * rows, width), F32), out((1, width), F32)],
        [(SMEM, odd), (VMEM, part), (VMEM, swapped(part, "dom", 1))],
    )
    return (output, feature_grad, weight_grad, bias_grad[0])


def solution(mesh):
    return jax.shard_map(
        on_device,
        mesh=mesh,
        in_specs=(
            P(None, "dom"),
            P(None, "hid"),
            P(None, "dom"),
            P(None, "dom"),
            P("dom", None, None),
            P("dom", None, None),
            P("dom", None, None),
            P("dom", None),
            P("hid"),
            P("hid", "dom"),
        ),
        out_specs=(P("hid", "dom"), P("hid", "dom"), P(None, "hid"), P("hid")),
        check_vma=False,
    )
```

```python
import functools

import jax
import jax.numpy as jnp
from jax import lax
from jax.experimental import pallas as pl
from jax.experimental.pallas import tpu as pltpu
from jax.sharding import PartitionSpec as P

TILE = 256
F32 = jnp.float32
BF16 = jnp.bfloat16
VMEM = pl.BlockSpec(memory_space=pltpu.VMEM)
SMEM = pl.BlockSpec(memory_space=pltpu.SMEM)
HBM = pl.BlockSpec(memory_space=pltpu.HBM)


def call(kernel, outs, operands, scratch=(), us=1, mib=16, place=VMEM):
    arrays = [array for _, array in operands]
    return pl.pallas_call(
        kernel,
        out_shape=tuple(outs),
        in_specs=[place for place, _ in operands],
        out_specs=tuple(place for _ in outs),
        scratch_shapes=scratch,
        compiler_params=pltpu.CompilerParams(vmem_limit_bytes=mib * 1024 * 1024),
        cost_estimate=pl.CostEstimate(flops=us * 1000**3, bytes_accessed=1, transcendentals=0),
    )(*arrays)


def out(shape, dtype):
    return jax.ShapeDtypeStruct(shape, dtype)


def shifted(block, axis, distance):
    size = lax.axis_size(axis)
    return lax.ppermute(block, axis, [((i + distance) % size, i) for i in range(size)])


def swapped(block, axis, bit):
    size = lax.axis_size(axis)
    return lax.ppermute(block, axis, [(i, i ^ bit) for i in range(size)])


def dot(a, b):
    return jnp.dot(a, b, preferred_element_type=F32)


def slots_by_nodes(hot, rows_t, nodes, first, count):
    slots = rows_t.shape[0]
    lanes = lax.broadcasted_iota(jnp.int32, (slots, nodes), 1)
    for p in range(first, first + count):
        hot[p * slots : (p + 1) * slots, :] = jnp.where(
            rows_t[:, p : p + 1] == lanes, 1.0, 0.0
        ).astype(BF16)


def nodes_by_slots(hot, rows, nodes):
    peers, slots = rows.shape
    lines = lax.broadcasted_iota(jnp.int32, (nodes, slots), 0)
    for p in range(peers):
        hot[:, p * slots : (p + 1) * slots] = jnp.where(
            rows[p : p + 1, :] == lines, 1.0, 0.0
        ).astype(BF16)


def masked_weights(weight, counts):
    slots = lax.broadcasted_iota(jnp.int32, weight.shape, 1)
    return jnp.where(slots < counts, weight, 0.0)


class Copies:
    def __init__(self, sems):
        self.sems, self.started = sems, []

    def start(self, source, target):
        copy = pltpu.make_async_copy(source, target, self.sems.at[len(self.started)])
        copy.start()
        self.started.append(copy)
        return copy


def vmem(shape, dtype):
    return pltpu.VMEM(shape, dtype)


def sems(count):
    return pltpu.SemaphoreType.DMA((count,))


def gather_kernel(hid_ref, features_ref, send_ref, out_ref, hot, block, lists, picked, sems):
    peers, slots, rows = out_ref.shape
    nodes = features_ref.shape[1]
    copies = Copies(sems)
    start = pl.multiple_of(hid_ref[0] * rows, rows)
    lists_copy = copies.start(send_ref, lists)
    block_copy = copies.start(features_ref.at[pl.ds(start, rows), :], block)
    lists_copy.wait()
    send_t = lists[...].T
    group = 4
    slots_by_nodes(hot, send_t, nodes, 0, group)
    block_copy.wait()
    sent = []
    block_t = block[...].T
    for p in range(0, peers, group):
        part = dot(hot[p * slots : (p + group) * slots, :], block_t)
        picked[p : p + group] = part.astype(BF16).reshape(group, slots, rows)
        sent.append(copies.start(picked.at[pl.ds(p, group)], out_ref.at[pl.ds(p, group)]))
        if p + group < peers:
            slots_by_nodes(hot, send_t, nodes, p + group, group)
    for copy in sent:
        copy.wait()


def live_lines(live_ref, s, i, side, axis):
    shape = (1, side * TILE) if axis else (side * TILE, 1)
    place = lax.broadcasted_iota(jnp.int32, shape, axis) // TILE
    live = jnp.zeros(shape, F32)
    for j in range(side):
        live = jnp.where(place == j, live_ref[s * side + j, i].astype(F32), live)
    return live.astype(BF16)


def dense_forward(live_ref, tiles_ref, block_ref, s, i, first):
    nodes = block_ref.shape[1]
    side = nodes // TILE
    left = block_ref[...] * live_lines(live_ref, s, i, side, 1)
    return dot(left, tiles_ref[first : first + nodes, i * TILE : (i + 1) * TILE])


def dense_kernel(live_ref, tiles_ref, before_ref, own_ref, after_ref, out_ref):
    nodes = out_ref.shape[0]
    for i in range(nodes // TILE):
        total = None
        for s, ref in enumerate((before_ref, own_ref, after_ref)):
            term = dense_forward(live_ref, tiles_ref, ref, s, i, s * nodes)
            total = term if total is None else total + term
        out_ref[i * TILE : (i + 1) * TILE, :] = total.T


def aggregate_kernel(recv_ref, weight_ref, counts_ref, arrived_ref, out_ref, hot, weighted):
    peers, slots, _ = arrived_ref.shape
    nodes_by_slots(hot, recv_ref[...], out_ref.shape[0])
    weights_t = masked_weights(weight_ref[...], counts_ref[...]).T
    for p in range(peers):
        row = arrived_ref[p].astype(F32) * weights_t[:, p : p + 1]
        weighted[p * slots : (p + 1) * slots, :] = row.astype(BF16)
    out_ref[...] = dot(hot[...], weighted[...])


def dense_backward(live_ref, tiles, block, s, first):
    nodes = block.shape[0]
    side = nodes // TILE
    place = lax.broadcasted_iota(jnp.int32, (nodes, 1), 0) // TILE
    for j in range(side):
        live = jnp.zeros((nodes, 1), F32)
        for i in range(side):
            live = jnp.where(place == i, live_ref[s * side + j, i].astype(F32), live)
        row = first + j * TILE
        yield j, dot(tiles[row : row + TILE, :], block * live.astype(BF16))


def dense_backward_kernel(parts, live_ref, tiles_ref, back_ref, *out_refs):
    nodes = back_ref.shape[0]
    for s, out_ref in zip(parts, out_refs):
        for j, term in dense_backward(live_ref, tiles_ref, back_ref[...], s, s * nodes):
            out_ref[j * TILE : (j + 1) * TILE, :] = term.astype(out_ref.dtype)


def weight_parts(hid_ref, grad, aggs, part_ref):
    n_hid, _, rows = aggs.shape
    for k in range(n_hid):
        start = pl.multiple_of(lax.rem(hid_ref[0] + k, n_hid) * rows, rows)
        part_ref[pl.ds(start, rows), :] = dot(aggs[k].T, grad)
    total = jnp.sum(grad.astype(F32), axis=0, keepdims=True)
    size = n_hid * rows
    part_ref[size:, :] = jnp.broadcast_to(total, (part_ref.shape[0] - size, part_ref.shape[1]))


def layer_kernel(n_hid, hid_ref, *refs):
    take = iter(refs)
    weights, biases, cotangents = ([next(take) for _ in range(n_hid)] for _ in range(3))
    aggs, output_ref, part_ref, back_ref, held, sems = take
    copies = Copies(sems)
    cotangents_in = [copies.start(ref, held.at[k]) for k, ref in enumerate(cotangents)]
    width, nodes = output_ref.shape
    rows = back_ref.shape[1]
    own = pl.ds(pl.multiple_of(hid_ref[0] * rows, rows), rows)
    total = None
    for k in range(n_hid):
        act = jnp.broadcast_to(biases[k][...], (nodes, width))
        for j in range(n_hid):
            start = pl.multiple_of(lax.rem(hid_ref[0] + j, n_hid) * rows, rows)
            act = act + dot(aggs[j], weights[k][pl.ds(start, rows), :])
        gate = 1.0 / (1.0 + jnp.exp(-act))
        slope = gate * (1.0 + act * (1.0 - gate))
        cotangents_in[k].wait()
        grad = (held[k].T.astype(F32) * slope).astype(BF16)
        if k == 0:
            output_ref[...] = (act * gate).astype(BF16).T
            weight_parts(hid_ref, grad, aggs, part_ref)
        term = lax.dot_general(
            grad, weights[k][own, :], (((1,), (1,)), ((), ())), preferred_element_type=F32
        )
        total = term if total is None else total + term
    back_ref[...] = total.astype(BF16)


def message_kernel(recv_ref, weight_ref, counts_ref, back_ref, message_ref, hot):
    peers, slots, _ = message_ref.shape
    back = back_ref[...]
    nodes = back.shape[0]
    weights_t = masked_weights(weight_ref[...], counts_ref[...]).T
    recv_t = recv_ref[...].T
    group = 4
    for p in range(0, peers, group):
        slots_by_nodes(hot, recv_t, nodes, p, group)
        picked = dot(hot[p * slots : (p + group) * slots, :], back)
        for n in range(group):
            row = picked[n * slots : (n + 1) * slots] * weights_t[:, p + n : p + n + 1]
            message_ref[p + n] = row.astype(BF16)


def joined_kernel(odd_ref, mine_ref, other_ref, weight_ref, bias_ref):
    half = mine_ref.shape[0]
    odd = odd_ref[0] == 1
    low = jnp.where(odd, other_ref[...], mine_ref[...])
    high = jnp.where(odd, mine_ref[...], other_ref[...])
    size = weight_ref.shape[0]
    weight_ref[:half, :] = low
    weight_ref[half:, :] = high[: size - half, :]
    bias_ref[...] = high[size - half : size - half + 1, :]


def scatter_kernel(send_ref, returned_ref, dense_ref, out_ref, hot):
    peers, slots, rows = returned_ref.shape
    nodes_by_slots(hot, send_ref[...], dense_ref.shape[0])
    returned = returned_ref[...].reshape(peers * slots, rows)
    total = dense_ref[...] + dot(hot[...], returned)
    out_ref[...] = total.astype(BF16).T


def halved(part, axis, bits):
    place = lax.axis_index(axis)
    for bit in bits:
        odd = lax.rem(place // bit, 2) == 1
        half = part.shape[0] // 2
        low, high = part[:half], part[half:]
        arrived = swapped(jnp.where(odd, low, high).astype(BF16), axis, bit)
        part = jnp.where(odd, high, low) + arrived.astype(F32)
    return part


def sum_kernel(mine_ref, other_ref, out_ref):
    out_ref[...] = mine_ref[...].astype(F32) + other_ref[...].astype(F32)


def doubled(part, axis, bits, us=1):
    for bit in bits:
        sent = part.astype(BF16)
        (part,) = call(
            sum_kernel, [out(part.shape, F32)], [(VMEM, sent), (VMEM, swapped(sent, axis, bit))], us=us
        )
    return part


def paired(mine, other, odd):
    return jnp.where(odd == 1, jnp.concatenate([other, mine]), jnp.concatenate([mine, other]))


def on_device(
    features,
    weight,
    band_tiles,
    tile_live,
    send_rows,
    recv_rows,
    edge_weight,
    live_slots,
    bias_terms,
    cotangent,
):
    n_hid = lax.axis_size("hid")
    hid = (SMEM, lax.axis_index("hid").astype(jnp.int32).reshape(1))
    peers, slots = send_rows.shape[1:]
    nodes = features.shape[1]
    width = weight.shape[1]
    rows = features.shape[0] // n_hid
    lists = peers * slots
    send, recv = (VMEM, send_rows[0]), (VMEM, recv_rows[0])
    edges = [recv, (VMEM, edge_weight[0]), (VMEM, live_slots.reshape(peers, 1))]
    tiles = [(SMEM, tile_live), (VMEM, band_tiles)]
    steps = range(1, n_hid)

    own = lax.dynamic_slice_in_dim(features, hid[1][0] * rows, rows, 0)
    before, after = shifted(own, "dom", -1), shifted(own, "dom", 1)
    (outgoing,) = call(
        gather_kernel,
        [out((peers, slots, rows), BF16)],
        [hid, (HBM, features), (HBM, send_rows[0])],
        [
            vmem((lists, nodes), BF16),
            vmem((rows, nodes), BF16),
            vmem((peers, slots), jnp.int32),
            vmem((peers, slots, rows), BF16),
            sems(peers + 2),
        ],
        mib=58,
        place=HBM,
    )
    arrived = lax.all_to_all(outgoing, "dom", split_axis=0, concat_axis=0, tiled=True)

    before, weight, bias_terms, cotangent = lax.optimization_barrier(
        (before, weight, bias_terms, cotangent)
    )
    weights = [weight] + [shifted(weight, "hid", k) for k in steps]
    biases = [bias_terms] + [shifted(bias_terms, "hid", k) for k in steps]
    cotangents = [cotangent] + [shifted(cotangent, "hid", k) for k in steps]
    (dense,) = call(
        dense_kernel,
        [out((nodes, rows), F32)],
        [*tiles, (VMEM, before), (VMEM, own), (VMEM, after)],
        us=60,
    )
    dense, weights, biases, cotangents = lax.optimization_barrier((dense, weights, biases, cotangents))
    (sparse,) = call(
        aggregate_kernel,
        [out((nodes, rows), F32)],
        [*edges, (VMEM, arrived)],
        [vmem((nodes, lists), BF16), vmem((lists, rows), BF16)],
        us=4,
    )
    agg = (dense + sparse).astype(BF16)
    aggs = jnp.stack([agg] + [shifted(agg, "hid", k) for k in steps])
    bits = [1 << b for b in range((peers - 1).bit_length())]
    pad = 64
    output, part, back = call(
        functools.partial(layer_kernel, n_hid),
        [
            out((width, nodes), BF16),
            out((n_hid * rows + pad, width), F32),
            out((nodes, rows), BF16),
        ],
        [
            hid,
            *[(VMEM, w) for w in weights],
            *[(VMEM, b[None, :]) for b in biases],
            *[(HBM, c) for c in cotangents],
            (VMEM, aggs),
        ],
        [vmem((n_hid, width, nodes), BF16), sems(n_hid)],
        us=2,
    )
    (message,) = call(
        message_kernel,
        [out((peers, slots, rows), BF16)],
        [*edges, (VMEM, back)],
        [vmem((lists, nodes), BF16)],
        us=2,
    )
    part = halved(part, "dom", bits[:1])
    message, part, back = lax.optimization_barrier((message, part, back))
    returned = lax.all_to_all(message, "dom", split_axis=0, concat_axis=0, tiled=True)

    to_before, to_after = call(
        functools.partial(dense_backward_kernel, (0, 2)),
        [out((nodes, rows), BF16)] * 2,
        [*tiles, (VMEM, back)],
    )
    (kept,) = call(
        functools.partial(dense_backward_kernel, (1,)),
        [out((nodes, rows), F32)],
        [*tiles, (VMEM, back)],
    )
    part = halved(part, "dom", bits[1:2])
    part, to_before, to_after = lax.optimization_barrier((part, to_before, to_after))
    from_after, from_before = shifted(to_before, "dom", 1), shifted(to_after, "dom", -1)
    part = doubled(part, "dom", bits[2:3], 5)
    part, kept = lax.optimization_barrier((part, kept))
    part = doubled(part, "dom", bits[3:])
    base = kept + from_after.astype(F32) + from_before.astype(F32)
    (feature_grad,) = call(
        scatter_kernel,
        [out((rows, nodes), BF16)],
        [send, (VMEM, returned), (VMEM, base)],
        [vmem((nodes, lists), BF16)],
    )
    place = lax.axis_index("dom")
    far = swapped(part, "dom", 2)
    far, feature_grad = lax.optimization_barrier((far, feature_grad))
    part = paired(part, far, place // 2 % 2)
    other = swapped(part, "dom", 1)
    weight_grad, bias_grad = call(
        joined_kernel,
        [out((n_hid * rows, width), F32), out((1, width), F32)],
        [(SMEM, (place % 2).astype(jnp.int32).reshape(1)), (VMEM, part), (VMEM, other)],
    )
    return (output, feature_grad, weight_grad, bias_grad[0])


def solution(mesh):
    return jax.shard_map(
        on_device,
        mesh=mesh,
        in_specs=(
            P(None, "dom"),
            P(None, "hid"),
            P(None, "dom"),
            P(None, "dom"),
            P("dom", None, None),
            P("dom", None, None),
            P("dom", None, None),
            P("dom", None),
            P("hid"),
            P("hid", "dom"),
        ),
        out_specs=(P("hid", "dom"), P("hid", "dom"), P(None, "hid"), P("hid")),
        check_vma=False,
    )
```

```python
import functools

import jax
import jax.numpy as jnp
from jax import lax
from jax.experimental import pallas as pl
from jax.experimental.pallas import tpu as pltpu
from jax.sharding import PartitionSpec as P

TILE = 256
F32 = jnp.float32
BF16 = jnp.bfloat16
VMEM = pl.BlockSpec(memory_space=pltpu.VMEM)
SMEM = pl.BlockSpec(memory_space=pltpu.SMEM)
HBM = pl.BlockSpec(memory_space=pltpu.HBM)


def call(kernel, outs, operands, scratch=(), us=1, mib=16, place=VMEM):
    arrays = [array for _, array in operands]
    return pl.pallas_call(
        kernel,
        out_shape=tuple(outs),
        in_specs=[place for place, _ in operands],
        out_specs=tuple(place) if isinstance(place, list) else tuple(place for _ in outs),
        scratch_shapes=scratch,
        compiler_params=pltpu.CompilerParams(vmem_limit_bytes=mib * 1024 * 1024),
        cost_estimate=pl.CostEstimate(flops=us * 1000**3, bytes_accessed=1, transcendentals=0),
    )(*arrays)


def out(shape, dtype):
    return jax.ShapeDtypeStruct(shape, dtype)


def shifted(block, axis, distance):
    size = lax.axis_size(axis)
    return lax.ppermute(block, axis, [((i + distance) % size, i) for i in range(size)])


def swapped(block, axis, bit):
    size = lax.axis_size(axis)
    return lax.ppermute(block, axis, [(i, i ^ bit) for i in range(size)])


def dot(a, b):
    return jnp.dot(a, b, preferred_element_type=F32)


def slots_by_nodes(hot, rows_t, first_node, first, count):
    slots = rows_t.shape[0]
    lanes = lax.broadcasted_iota(jnp.int32, (slots, hot.shape[1]), 1) + first_node
    for p in range(first, first + count):
        hot[p * slots : (p + 1) * slots, :] = jnp.where(
            rows_t[:, p : p + 1] == lanes, 1.0, 0.0
        ).astype(BF16)


def nodes_by_slots(hot, rows, nodes):
    peers, slots = rows.shape
    lines = lax.broadcasted_iota(jnp.int32, (nodes, slots), 0)
    for p in range(peers):
        hot[:, p * slots : (p + 1) * slots] = jnp.where(
            rows[p : p + 1, :] == lines, 1.0, 0.0
        ).astype(BF16)


def masked_weights(weight, counts):
    slots = lax.broadcasted_iota(jnp.int32, weight.shape, 1)
    return jnp.where(slots < counts, weight, 0.0)


class Copies:
    def __init__(self, sems):
        self.sems, self.started = sems, []

    def start(self, source, target):
        copy = pltpu.make_async_copy(source, target, self.sems.at[len(self.started)])
        copy.start()
        self.started.append(copy)
        return copy


def vmem(shape, dtype):
    return pltpu.VMEM(shape, dtype)


def sems(count):
    return pltpu.SemaphoreType.DMA((count,))


def gather_kernel(hid_ref, features_ref, send_ref, out_ref, hot, block, lists, picked, sems):
    peers, slots, rows = out_ref.shape
    nodes = features_ref.shape[1]
    copies = Copies(sems)
    start = pl.multiple_of(hid_ref[0] * rows, rows)
    lists_copy = copies.start(send_ref, lists)
    block_copy = copies.start(features_ref.at[pl.ds(start, rows), :], block)
    lists_copy.wait()
    send_t = lists[...].T
    group = 2
    slots_by_nodes(hot, send_t, 0, 0, group)
    block_copy.wait()
    sent = []
    block_t = block[...].T
    for p in range(0, peers, group):
        part = dot(hot[p * slots : (p + group) * slots, :], block_t)
        picked[p : p + group] = part.astype(BF16).reshape(group, slots, rows)
        sent.append(copies.start(picked.at[pl.ds(p, group)], out_ref.at[pl.ds(p, group)]))
        if p + group < peers:
            slots_by_nodes(hot, send_t, 0, p + group, group)
    for copy in sent:
        copy.wait()


def live_lines(live_ref, s, i, side, axis):
    shape = (1, side * TILE) if axis else (side * TILE, 1)
    place = lax.broadcasted_iota(jnp.int32, shape, axis) // TILE
    live = jnp.zeros(shape, F32)
    for j in range(side):
        live = jnp.where(place == j, live_ref[s * side + j, i].astype(F32), live)
    return live.astype(BF16)


def dense_forward(live_ref, tiles_ref, block_ref, s, i, first):
    nodes = block_ref.shape[1]
    side = nodes // TILE
    left = block_ref[...] * live_lines(live_ref, s, i, side, 1)
    return dot(left, tiles_ref[first : first + nodes, i * TILE : (i + 1) * TILE])


def dense_kernel(live_ref, tiles_ref, before_ref, own_ref, after_ref, out_ref):
    nodes = out_ref.shape[0]
    for i in range(nodes // TILE):
        total = None
        for s, ref in enumerate((before_ref, own_ref, after_ref)):
            term = dense_forward(live_ref, tiles_ref, ref, s, i, s * nodes)
            total = term if total is None else total + term
        out_ref[i * TILE : (i + 1) * TILE, :] = total.T


def aggregate_kernel(recv_ref, weight_ref, counts_ref, arrived_ref, out_ref, hot, weighted):
    peers, slots, _ = arrived_ref.shape
    nodes_by_slots(hot, recv_ref[...], out_ref.shape[0])
    weights_t = masked_weights(weight_ref[...], counts_ref[...]).T
    for p in range(peers):
        row = arrived_ref[p].astype(F32) * weights_t[:, p : p + 1]
        weighted[p * slots : (p + 1) * slots, :] = row.astype(BF16)
    out_ref[...] = dot(hot[...], weighted[...])


def dense_backward(live_ref, tiles, block, s, first):
    nodes = block.shape[0]
    side = nodes // TILE
    place = lax.broadcasted_iota(jnp.int32, (nodes, 1), 0) // TILE
    for j in range(side):
        live = jnp.zeros((nodes, 1), F32)
        for i in range(side):
            live = jnp.where(place == i, live_ref[s * side + j, i].astype(F32), live)
        row = first + j * TILE
        yield j, dot(tiles[row : row + TILE, :], block * live.astype(BF16))


def dense_backward_kernel(parts, live_ref, tiles_ref, back_ref, *out_refs):
    nodes = back_ref.shape[0]
    for s, out_ref in zip(parts, out_refs):
        for j, term in dense_backward(live_ref, tiles_ref, back_ref[...], s, s * nodes):
            out_ref[j * TILE : (j + 1) * TILE, :] = term.astype(out_ref.dtype)


def weight_parts(hid_ref, grad, aggs, part_ref):
    n_hid, _, rows = aggs.shape
    for k in range(n_hid):
        start = pl.multiple_of(lax.rem(hid_ref[0] + k, n_hid) * rows, rows)
        part_ref[pl.ds(start, rows), :] = dot(aggs[k].T, grad)
    total = jnp.sum(grad.astype(F32), axis=0, keepdims=True)
    size = n_hid * rows
    part_ref[size:, :] = jnp.broadcast_to(total, (part_ref.shape[0] - size, part_ref.shape[1]))


def layer_kernel(n_hid, first, hid_ref, *refs):
    take = iter(refs)
    weights, biases, cotangents = ([next(take) for _ in range(n_hid)] for _ in range(3))
    aggs, recv_ref, weight_ref, counts_ref = (next(take) for _ in range(4))
    earlier_ref = next(take) if first else None
    output_ref, part_ref, back_ref, message_ref, held, earlier, hot, sems = take
    copies = Copies(sems)
    earlier_in = copies.start(earlier_ref, earlier) if first else None
    width, nodes = output_ref.shape
    rows = back_ref.shape[1]
    cotangents_in = [
        copies.start(ref.at[:, pl.ds(first, nodes)], held.at[k]) for k, ref in enumerate(cotangents)
    ]
    own = pl.ds(pl.multiple_of(hid_ref[0] * rows, rows), rows)
    total = None
    for k in range(n_hid):
        act = jnp.broadcast_to(biases[k][...], (nodes, width))
        for j in range(n_hid):
            start = pl.multiple_of(lax.rem(hid_ref[0] + j, n_hid) * rows, rows)
            act = act + dot(aggs[j], weights[k][pl.ds(start, rows), :])
        gate = 1.0 / (1.0 + jnp.exp(-act))
        slope = gate * (1.0 + act * (1.0 - gate))
        cotangents_in[k].wait()
        grad = (held[k].T.astype(F32) * slope).astype(BF16)
        if k == 0:
            output_ref[...] = (act * gate).astype(BF16).T
            weight_parts(hid_ref, grad, aggs, part_ref)
        term = lax.dot_general(
            grad, weights[k][own, :], (((1,), (1,)), ((), ())), preferred_element_type=F32
        )
        total = term if total is None else total + term
    back_ref[...] = total.astype(BF16)
    back = back_ref[...]
    peers, slots, _ = message_ref.shape
    weights_t = masked_weights(weight_ref[...], counts_ref[...]).T
    recv_t = recv_ref[...].T
    if first:
        earlier_in.wait()
    sent = []
    group = 4
    for p in range(0, peers, group):
        slots_by_nodes(hot, recv_t, first, p, group)
        picked = dot(hot[p * slots : (p + group) * slots, :], back)
        for n in range(group):
            row = picked[n * slots : (n + 1) * slots] * weights_t[:, p + n : p + n + 1]
            if first:
                row = row + earlier[p + n].astype(F32)
            earlier[p + n] = row.astype(BF16)
        lines = pl.ds(p, group)
        sent.append(copies.start(earlier.at[lines], message_ref.at[lines]))
    for copy in sent:
        copy.wait()


def joined_kernel(odd_ref, mine_ref, other_ref, weight_ref, bias_ref):
    half = mine_ref.shape[0]
    odd = odd_ref[0] == 1
    low = jnp.where(odd, other_ref[...], mine_ref[...])
    high = jnp.where(odd, mine_ref[...], other_ref[...])
    size = weight_ref.shape[0]
    weight_ref[:half, :] = low
    weight_ref[half:, :] = high[: size - half, :]
    bias_ref[...] = high[size - half : size - half + 1, :]


def scatter_kernel(send_ref, returned_ref, dense_ref, out_ref, hot):
    peers, slots, rows = returned_ref.shape
    nodes_by_slots(hot, send_ref[...], dense_ref.shape[0])
    returned = returned_ref[...].reshape(peers * slots, rows)
    total = dense_ref[...] + dot(hot[...], returned)
    out_ref[...] = total.astype(BF16).T


def halved(part, axis, bits):
    place = lax.axis_index(axis)
    for bit in bits:
        odd = lax.rem(place // bit, 2) == 1
        half = part.shape[0] // 2
        low, high = part[:half], part[half:]
        arrived = swapped(jnp.where(odd, low, high).astype(BF16), axis, bit)
        part = jnp.where(odd, high, low) + arrived.astype(F32)
    return part


def exchanged(part, axis, bits):
    while bits:
        sent, near, bits = part.astype(BF16), bits[0], bits[1:]
        part = sent.astype(F32) + swapped(sent, axis, near).astype(F32)
        if bits:
            far, bits = bits[0], bits[1:]
            others = [swapped(sent, axis, bit).astype(F32) for bit in (far, far ^ near)]
            part = part + (others[0] + others[1])
    return part


def paired(mine, other, odd):
    return jnp.where(odd == 1, jnp.concatenate([other, mine]), jnp.concatenate([mine, other]))


def on_device(
    features,
    weight,
    band_tiles,
    tile_live,
    send_rows,
    recv_rows,
    edge_weight,
    live_slots,
    bias_terms,
    cotangent,
):
    n_hid = lax.axis_size("hid")
    hid = (SMEM, lax.axis_index("hid").astype(jnp.int32).reshape(1))
    peers, slots = send_rows.shape[1:]
    nodes = features.shape[1]
    width = weight.shape[1]
    rows = features.shape[0] // n_hid
    lists = peers * slots
    send, recv = (VMEM, send_rows[0]), (VMEM, recv_rows[0])
    edges = [recv, (VMEM, edge_weight[0]), (VMEM, live_slots.reshape(peers, 1))]
    tiles = [(SMEM, tile_live), (VMEM, band_tiles)]
    steps = range(1, n_hid)

    own = lax.dynamic_slice_in_dim(features, hid[1][0] * rows, rows, 0)
    before, after = shifted(own, "dom", -1), shifted(own, "dom", 1)
    (outgoing,) = call(
        gather_kernel,
        [out((peers, slots, rows), BF16)],
        [hid, (HBM, features), (HBM, send_rows[0])],
        [
            vmem((lists, nodes), BF16),
            vmem((rows, nodes), BF16),
            vmem((peers, slots), jnp.int32),
            vmem((peers, slots, rows), BF16),
            sems(peers + 2),
        ],
        mib=58,
        place=HBM,
    )
    arrived = lax.all_to_all(outgoing, "dom", split_axis=0, concat_axis=0, tiled=True)

    before, weight, bias_terms, cotangent = lax.optimization_barrier(
        (before, weight, bias_terms, cotangent)
    )
    weights = [weight] + [shifted(weight, "hid", k) for k in steps]
    biases = [bias_terms] + [shifted(bias_terms, "hid", k) for k in steps]
    cotangents = [cotangent] + [shifted(cotangent, "hid", k) for k in steps]
    (dense,) = call(
        dense_kernel,
        [out((nodes, rows), F32)],
        [*tiles, (VMEM, before), (VMEM, own), (VMEM, after)],
        us=60,
    )
    dense, weights, biases, cotangents = lax.optimization_barrier((dense, weights, biases, cotangents))
    (sparse,) = call(
        aggregate_kernel,
        [out((nodes, rows), F32)],
        [*edges, (VMEM, arrived)],
        [vmem((nodes, lists), BF16), vmem((lists, rows), BF16)],
        us=4,
    )
    bits = [1 << b for b in range((peers - 1).bit_length())]
    pad = 64
    cuts = 2
    size = nodes // cuts
    outputs, parts, backs, message = [], [], [], None
    for cut in range(cuts):
        lines = slice(cut * size, (cut + 1) * size)
        agg = (dense[lines] + sparse[lines]).astype(BF16)
        others = [shifted(agg, "hid", k) for k in steps]
        if backs:
            agg, _ = lax.optimization_barrier((agg, backs[-1]))
        aggs = jnp.stack([agg] + others)
        output, part, back, message = call(
            functools.partial(layer_kernel, n_hid, cut * size),
            [
                out((width, size), BF16),
                out((n_hid * rows + pad, width), F32),
                out((size, rows), BF16),
                out((peers, slots, rows), BF16),
            ],
            [
                hid,
                *[(VMEM, w) for w in weights],
                *[(VMEM, b[None, :]) for b in biases],
                *[(HBM, c) for c in cotangents],
                (VMEM, aggs),
                *edges,
                *([(HBM, message)] if cut else []),
            ],
            [
                vmem((n_hid, width, size), BF16),
                vmem((peers, slots, rows), BF16),
                vmem((lists, size), BF16),
                sems(n_hid + 1 + peers),
            ],
            us=2,
            mib=24,
            place=[VMEM, VMEM, VMEM, HBM],
        )
        outputs.append(output)
        parts.append(part)
        backs.append(back)
    part = sum(parts[1:], parts[0])
    part = halved(part, "dom", bits[:1])
    back = jnp.concatenate(backs)
    to_before, to_after = call(
        functools.partial(dense_backward_kernel, (0, 2)),
        [out((nodes, rows), BF16)] * 2,
        [*tiles, (VMEM, back)],
        us=2,
    )
    from_after, from_before = shifted(to_before, "dom", 1), shifted(to_after, "dom", -1)
    message, _ = lax.optimization_barrier((message, to_before))
    returned = lax.all_to_all(message, "dom", split_axis=0, concat_axis=0, tiled=True)
    (kept,) = call(
        functools.partial(dense_backward_kernel, (1,)),
        [out((nodes, rows), F32)],
        [*tiles, (VMEM, back)],
    )
    part = halved(part, "dom", bits[1:2])
    part, to_before, to_after = lax.optimization_barrier((part, to_before, to_after))
    part = exchanged(part, "dom", bits[2:])
    place = lax.axis_index("dom")
    far = swapped(part, "dom", 2)
    part = paired(part, far, place // 2 % 2)
    output = jnp.concatenate(outputs, axis=1)
    part, output, kept, from_before, from_after = lax.optimization_barrier(
        (part, output, kept, from_before, from_after)
    )
    base = kept + from_before.astype(F32) + from_after.astype(F32)
    other = swapped(part, "dom", 1)
    weight_grad, bias_grad = call(
        joined_kernel,
        [out((n_hid * rows, width), F32), out((1, width), F32)],
        [(SMEM, (place % 2).astype(jnp.int32).reshape(1)), (VMEM, part), (VMEM, other)],
        us=15,
    )
    (feature_grad,) = call(
        scatter_kernel,
        [out((rows, nodes), BF16)],
        [send, (VMEM, returned), (VMEM, base)],
        [vmem((nodes, lists), BF16)],
    )
    return (output, feature_grad, weight_grad, bias_grad[0])


def solution(mesh):
    return jax.shard_map(
        on_device,
        mesh=mesh,
        in_specs=(
            P(None, "dom"),
            P(None, "hid"),
            P(None, "dom"),
            P(None, "dom"),
            P("dom", None, None),
            P("dom", None, None),
            P("dom", None, None),
            P("dom", None),
            P("hid"),
            P("hid", "dom"),
        ),
        out_specs=(P("hid", "dom"), P("hid", "dom"), P(None, "hid"), P("hid")),
        check_vma=False,
    )
```

```python
import functools

import jax
import jax.numpy as jnp
from jax import lax
from jax.experimental import pallas as pl
from jax.experimental.pallas import tpu as pltpu
from jax.sharding import PartitionSpec as P

TILE = 256
F32 = jnp.float32
BF16 = jnp.bfloat16
VMEM = pl.BlockSpec(memory_space=pltpu.VMEM)
SMEM = pl.BlockSpec(memory_space=pltpu.SMEM)
HBM = pl.BlockSpec(memory_space=pltpu.HBM)


def call(kernel, outs, operands, scratch=(), us=1, mib=16, place=VMEM):
    arrays = [array for _, array in operands]
    return pl.pallas_call(
        kernel,
        out_shape=tuple(outs),
        in_specs=[place for place, _ in operands],
        out_specs=tuple(place) if isinstance(place, list) else tuple(place for _ in outs),
        scratch_shapes=scratch,
        compiler_params=pltpu.CompilerParams(vmem_limit_bytes=mib * 1024 * 1024),
        cost_estimate=pl.CostEstimate(flops=us * 1000**3, bytes_accessed=1, transcendentals=0),
    )(*arrays)


def out(shape, dtype):
    return jax.ShapeDtypeStruct(shape, dtype)


def shifted(block, axis, distance):
    size = lax.axis_size(axis)
    return lax.ppermute(block, axis, [((i + distance) % size, i) for i in range(size)])


def swapped(block, axis, bit):
    size = lax.axis_size(axis)
    return lax.ppermute(block, axis, [(i, i ^ bit) for i in range(size)])


def dot(a, b):
    return jnp.dot(a, b, preferred_element_type=F32)


def slots_by_nodes(hot, rows_t, first_node, first, count):
    slots = rows_t.shape[0]
    lanes = lax.broadcasted_iota(jnp.int32, (slots, hot.shape[1]), 1) + first_node
    for p in range(first, first + count):
        hot[p * slots : (p + 1) * slots, :] = jnp.where(
            rows_t[:, p : p + 1] == lanes, 1.0, 0.0
        ).astype(BF16)


def nodes_by_slots(hot, rows, nodes):
    peers, slots = rows.shape
    lines = lax.broadcasted_iota(jnp.int32, (nodes, slots), 0)
    for p in range(peers):
        hot[:, p * slots : (p + 1) * slots] = jnp.where(
            rows[p : p + 1, :] == lines, 1.0, 0.0
        ).astype(BF16)


def masked_weights(weight, counts):
    slots = lax.broadcasted_iota(jnp.int32, weight.shape, 1)
    return jnp.where(slots < counts, weight, 0.0)


class Copies:
    def __init__(self, sems):
        self.sems, self.started = sems, []

    def start(self, source, target):
        copy = pltpu.make_async_copy(source, target, self.sems.at[len(self.started)])
        copy.start()
        self.started.append(copy)
        return copy


def vmem(shape, dtype):
    return pltpu.VMEM(shape, dtype)


def sems(count):
    return pltpu.SemaphoreType.DMA((count,))


def gather_kernel(block_ref, send_ref, out_ref, hot, picked, sems):
    peers, slots, rows = out_ref.shape
    copies, sent = Copies(sems), []
    send_t = send_ref[...].T
    block_t = block_ref[...].T
    group = 2
    for p in range(0, peers, group):
        slots_by_nodes(hot, send_t, 0, p, group)
        part = dot(hot[p * slots : (p + group) * slots, :], block_t)
        picked[p : p + group] = part.astype(BF16).reshape(group, slots, rows)
        sent.append(copies.start(picked.at[pl.ds(p, group)], out_ref.at[pl.ds(p, group)]))
    for copy in sent:
        copy.wait()


def live_lines(live_ref, s, i, side, axis):
    shape = (1, side * TILE) if axis else (side * TILE, 1)
    place = lax.broadcasted_iota(jnp.int32, shape, axis) // TILE
    live = jnp.zeros(shape, F32)
    for j in range(side):
        live = jnp.where(place == j, live_ref[s * side + j, i].astype(F32), live)
    return live.astype(BF16)


def dense_forward(live_ref, tiles_ref, block_ref, s, i, first):
    nodes = block_ref.shape[1]
    side = nodes // TILE
    left = block_ref[...] * live_lines(live_ref, s, i, side, 1)
    return dot(left, tiles_ref[first : first + nodes, i * TILE : (i + 1) * TILE])


def dense_kernel(live_ref, tiles_ref, before_ref, own_ref, after_ref, out_ref):
    nodes = out_ref.shape[0]
    for i in range(nodes // TILE):
        total = None
        for s, ref in enumerate((before_ref, own_ref, after_ref)):
            term = dense_forward(live_ref, tiles_ref, ref, s, i, s * nodes)
            total = term if total is None else total + term
        out_ref[i * TILE : (i + 1) * TILE, :] = total.T


def aggregate_kernel(recv_ref, weight_ref, counts_ref, arrived_ref, out_ref, hot, weighted):
    peers, slots, _ = arrived_ref.shape
    nodes_by_slots(hot, recv_ref[...], out_ref.shape[0])
    weights_t = masked_weights(weight_ref[...], counts_ref[...]).T
    for p in range(peers):
        row = arrived_ref[p].astype(F32) * weights_t[:, p : p + 1]
        weighted[p * slots : (p + 1) * slots, :] = row.astype(BF16)
    out_ref[...] = dot(hot[...], weighted[...])


def dense_backward(live_ref, tiles, block, s, first):
    nodes = block.shape[0]
    side = nodes // TILE
    place = lax.broadcasted_iota(jnp.int32, (nodes, 1), 0) // TILE
    for j in range(side):
        live = jnp.zeros((nodes, 1), F32)
        for i in range(side):
            live = jnp.where(place == i, live_ref[s * side + j, i].astype(F32), live)
        row = first + j * TILE
        yield j, dot(tiles[row : row + TILE, :], block * live.astype(BF16))


def dense_backward_kernel(parts, live_ref, tiles_ref, back_ref, *out_refs):
    nodes = back_ref.shape[0]
    for s, out_ref in zip(parts, out_refs):
        for j, term in dense_backward(live_ref, tiles_ref, back_ref[...], s, s * nodes):
            out_ref[j * TILE : (j + 1) * TILE, :] = term.astype(out_ref.dtype)


def weight_parts(hid_ref, grad, aggs, part_ref):
    n_hid, _, rows = aggs.shape
    for k in range(n_hid):
        start = pl.multiple_of(lax.rem(hid_ref[0] + k, n_hid) * rows, rows)
        part_ref[pl.ds(start, rows), :] = dot(aggs[k].T, grad)
    total = jnp.sum(grad.astype(F32), axis=0, keepdims=True)
    size = n_hid * rows
    part_ref[size:, :] = jnp.broadcast_to(total, (part_ref.shape[0] - size, part_ref.shape[1]))


def layer_kernel(n_hid, first, hid_ref, *refs):
    take = iter(refs)
    weights, biases, cotangents = ([next(take) for _ in range(n_hid)] for _ in range(3))
    aggs, recv_ref, weight_ref, counts_ref = (next(take) for _ in range(4))
    earlier_ref = next(take) if first else None
    output_ref, part_ref, back_ref, message_ref, held, held_message, hot, sems = take
    copies = Copies(sems)
    width, nodes = output_ref.shape
    rows = back_ref.shape[1]
    cotangents_in = [
        copies.start(ref.at[:, pl.ds(first, nodes)], held.at[k]) for k, ref in enumerate(cotangents)
    ]
    own = pl.ds(pl.multiple_of(hid_ref[0] * rows, rows), rows)
    total = None
    for k in range(n_hid):
        act = jnp.broadcast_to(biases[k][...], (nodes, width))
        for j in range(n_hid):
            start = pl.multiple_of(lax.rem(hid_ref[0] + j, n_hid) * rows, rows)
            act = act + dot(aggs[j], weights[k][pl.ds(start, rows), :])
        gate = 1.0 / (1.0 + jnp.exp(-act))
        slope = gate * (1.0 + act * (1.0 - gate))
        cotangents_in[k].wait()
        grad = (held[k].T.astype(F32) * slope).astype(BF16)
        if k == 0:
            output_ref[...] = (act * gate).astype(BF16).T
            weight_parts(hid_ref, grad, aggs, part_ref)
        term = lax.dot_general(
            grad, weights[k][own, :], (((1,), (1,)), ((), ())), preferred_element_type=F32
        )
        total = term if total is None else total + term
    back_ref[...] = total.astype(BF16)
    back = back_ref[...]
    peers, slots, _ = message_ref.shape
    weights_t = masked_weights(weight_ref[...], counts_ref[...]).T
    recv_t = recv_ref[...].T
    group = 8
    sent = []
    for p in range(0, peers, group):
        slots_by_nodes(hot, recv_t, first, p, group)
        picked = dot(hot[p * slots : (p + group) * slots, :], back)
        for n in range(group):
            row = picked[n * slots : (n + 1) * slots] * weights_t[:, p + n : p + n + 1]
            if first:
                held_message[p + n] = (row + earlier_ref[p + n].astype(F32)).astype(BF16)
            else:
                message_ref[p + n] = row.astype(BF16)
        if first:
            lines = pl.ds(p, group)
            sent.append(copies.start(held_message.at[lines], message_ref.at[lines]))
    for copy in sent:
        copy.wait()


def joined_kernel(odd_ref, mine_ref, other_ref, weight_ref, bias_ref):
    half = mine_ref.shape[0]
    odd = odd_ref[0] == 1
    low = jnp.where(odd, other_ref[...], mine_ref[...])
    high = jnp.where(odd, mine_ref[...], other_ref[...])
    size = weight_ref.shape[0]
    weight_ref[:half, :] = low
    weight_ref[half:, :] = high[: size - half, :]
    bias_ref[...] = high[size - half : size - half + 1, :]


def scatter_kernel(send_ref, returned_ref, dense_ref, out_ref, hot):
    peers, slots, rows = returned_ref.shape
    nodes_by_slots(hot, send_ref[...], dense_ref.shape[0])
    returned = returned_ref[...].reshape(peers * slots, rows)
    total = dense_ref[...] + dot(hot[...], returned)
    out_ref[...] = total.astype(BF16).T


def halved(part, axis, bits):
    place = lax.axis_index(axis)
    for bit in bits:
        odd = lax.rem(place // bit, 2) == 1
        half = part.shape[0] // 2
        low, high = part[:half], part[half:]
        arrived = swapped(jnp.where(odd, low, high).astype(BF16), axis, bit)
        part = jnp.where(odd, high, low) + arrived.astype(F32)
    return part


def exchanged(part, axis, bits):
    while bits:
        sent, near, bits = part.astype(BF16), bits[0], bits[1:]
        part = sent.astype(F32) + swapped(sent, axis, near).astype(F32)
        if bits:
            far, bits = bits[0], bits[1:]
            others = [swapped(sent, axis, bit).astype(F32) for bit in (far, far ^ near)]
            part = part + (others[0] + others[1])
    return part


def paired(mine, other, odd):
    return jnp.where(odd == 1, jnp.concatenate([other, mine]), jnp.concatenate([mine, other]))


def on_device(
    features,
    weight,
    band_tiles,
    tile_live,
    send_rows,
    recv_rows,
    edge_weight,
    live_slots,
    bias_terms,
    cotangent,
):
    n_hid = lax.axis_size("hid")
    hid = (SMEM, lax.axis_index("hid").astype(jnp.int32).reshape(1))
    peers, slots = send_rows.shape[1:]
    nodes = features.shape[1]
    width = weight.shape[1]
    rows = features.shape[0] // n_hid
    lists = peers * slots
    send, recv = (VMEM, send_rows[0]), (VMEM, recv_rows[0])
    edges = [recv, (VMEM, edge_weight[0]), (VMEM, live_slots.reshape(peers, 1))]
    tiles = [(SMEM, tile_live), (VMEM, band_tiles)]
    steps = range(1, n_hid)

    own = lax.dynamic_slice_in_dim(features, hid[1][0] * rows, rows, 0)
    before, after = shifted(own, "dom", -1), shifted(own, "dom", 1)
    (outgoing,) = call(
        gather_kernel,
        [out((peers, slots, rows), BF16)],
        [(VMEM, own), send],
        [vmem((lists, nodes), BF16), vmem((peers, slots, rows), BF16), sems(peers)],
        place=HBM,
    )
    arrived = lax.all_to_all(outgoing, "dom", split_axis=0, concat_axis=0, tiled=True)

    before, weight, bias_terms, cotangent = lax.optimization_barrier(
        (before, weight, bias_terms, cotangent)
    )
    weights = [weight] + [shifted(weight, "hid", k) for k in steps]
    biases = [bias_terms] + [shifted(bias_terms, "hid", k) for k in steps]
    cotangents = [cotangent] + [shifted(cotangent, "hid", k) for k in steps]
    (dense,) = call(
        dense_kernel,
        [out((nodes, rows), F32)],
        [*tiles, (VMEM, before), (VMEM, own), (VMEM, after)],
        us=60,
    )
    dense, weights, biases, cotangents = lax.optimization_barrier((dense, weights, biases, cotangents))
    (sparse,) = call(
        aggregate_kernel,
        [out((nodes, rows), F32)],
        [*edges, (VMEM, arrived)],
        [vmem((nodes, lists), BF16), vmem((lists, rows), BF16)],
        us=4,
    )
    bits = [1 << b for b in range((peers - 1).bit_length())]
    pad = 64
    cuts = 2
    size = nodes // cuts
    outputs, parts, backs, message = [], [], [], None
    for cut in range(cuts):
        lines = slice(cut * size, (cut + 1) * size)
        agg = (dense[lines] + sparse[lines]).astype(BF16)
        others = [shifted(agg, "hid", k) for k in steps]
        if backs:
            agg, _ = lax.optimization_barrier((agg, backs[-1]))
        aggs = jnp.stack([agg] + others)
        output, part, back, message = call(
            functools.partial(layer_kernel, n_hid, cut * size),
            [
                out((width, size), BF16),
                out((n_hid * rows + pad, width), F32),
                out((size, rows), BF16),
                out((peers, slots, rows), BF16),
            ],
            [
                hid,
                *[(VMEM, w) for w in weights],
                *[(VMEM, b[None, :]) for b in biases],
                *[(HBM, c) for c in cotangents],
                (VMEM, aggs),
                *edges,
                *([(VMEM, message)] if cut else []),
            ],
            [
                vmem((n_hid, width, size), BF16),
                vmem((peers, slots, rows), BF16),
                vmem((lists, size), BF16),
                sems(n_hid + 1 + peers),
            ],
            us=2,
            mib=24,
            place=[VMEM, VMEM, VMEM, HBM if cut else VMEM],
        )
        outputs.append(output)
        parts.append(part)
        backs.append(back)
    part = sum(parts[1:], parts[0])
    part = halved(part, "dom", bits[:1])
    back = jnp.concatenate(backs)
    to_before, to_after = call(
        functools.partial(dense_backward_kernel, (0, 2)),
        [out((nodes, rows), BF16)] * 2,
        [*tiles, (VMEM, back)],
        us=2,
    )
    from_after, from_before = shifted(to_before, "dom", 1), shifted(to_after, "dom", -1)
    message, _ = lax.optimization_barrier((message, to_before))
    returned = lax.all_to_all(message, "dom", split_axis=0, concat_axis=0, tiled=True)
    (kept,) = call(
        functools.partial(dense_backward_kernel, (1,)),
        [out((nodes, rows), F32)],
        [*tiles, (VMEM, back)],
    )
    part = halved(part, "dom", bits[1:2])
    part, to_before, to_after = lax.optimization_barrier((part, to_before, to_after))
    part = exchanged(part, "dom", bits[2:])
    place = lax.axis_index("dom")
    far = swapped(part, "dom", 2)
    part = paired(part, far, place // 2 % 2)
    output = jnp.concatenate(outputs, axis=1)
    part, output, kept, from_before, from_after = lax.optimization_barrier(
        (part, output, kept, from_before, from_after)
    )
    base = kept + from_before.astype(F32) + from_after.astype(F32)
    other = swapped(part, "dom", 1)
    weight_grad, bias_grad = call(
        joined_kernel,
        [out((n_hid * rows, width), F32), out((1, width), F32)],
        [(SMEM, (place % 2).astype(jnp.int32).reshape(1)), (VMEM, part), (VMEM, other)],
        us=15,
    )
    (feature_grad,) = call(
        scatter_kernel,
        [out((rows, nodes), BF16)],
        [send, (VMEM, returned), (VMEM, base)],
        [vmem((nodes, lists), BF16)],
    )
    return (output, feature_grad, weight_grad, bias_grad[0])


def solution(mesh):
    return jax.shard_map(
        on_device,
        mesh=mesh,
        in_specs=(
            P(None, "dom"),
            P(None, "hid"),
            P(None, "dom"),
            P(None, "dom"),
            P("dom", None, None),
            P("dom", None, None),
            P("dom", None, None),
            P("dom", None),
            P("hid"),
            P("hid", "dom"),
        ),
        out_specs=(P("hid", "dom"), P("hid", "dom"), P(None, "hid"), P("hid")),
        check_vma=False,
    )
```

```python
import functools

import jax
import jax.numpy as jnp
from jax import lax
from jax.experimental import pallas as pl
from jax.experimental.pallas import tpu as pltpu
from jax.sharding import PartitionSpec as P

TILE = 256
F32 = jnp.float32
BF16 = jnp.bfloat16
VMEM = pl.BlockSpec(memory_space=pltpu.VMEM)
SMEM = pl.BlockSpec(memory_space=pltpu.SMEM)
HBM = pl.BlockSpec(memory_space=pltpu.HBM)


def call(kernel, outs, operands, scratch=(), us=1, mib=16, place=VMEM):
    arrays = [array for _, array in operands]
    return pl.pallas_call(
        kernel,
        out_shape=tuple(outs),
        in_specs=[place for place, _ in operands],
        out_specs=tuple(place) if isinstance(place, list) else tuple(place for _ in outs),
        scratch_shapes=scratch,
        compiler_params=pltpu.CompilerParams(vmem_limit_bytes=mib * 1024 * 1024),
        cost_estimate=pl.CostEstimate(flops=us * 1000**3, bytes_accessed=1, transcendentals=0),
    )(*arrays)


def out(shape, dtype):
    return jax.ShapeDtypeStruct(shape, dtype)


def shifted(block, axis, distance):
    size = lax.axis_size(axis)
    return lax.ppermute(block, axis, [((i + distance) % size, i) for i in range(size)])


def swapped(block, axis, bit):
    size = lax.axis_size(axis)
    return lax.ppermute(block, axis, [(i, i ^ bit) for i in range(size)])


def dot(a, b):
    return jnp.dot(a, b, preferred_element_type=F32)


def slots_by_nodes(hot, rows_t, first_node, first, count):
    slots = rows_t.shape[0]
    lanes = lax.broadcasted_iota(jnp.int32, (slots, hot.shape[1]), 1) + first_node
    for p in range(first, first + count):
        hot[p * slots : (p + 1) * slots, :] = jnp.where(
            rows_t[:, p : p + 1] == lanes, 1.0, 0.0
        ).astype(BF16)


def nodes_by_slots(hot, rows, nodes):
    peers, slots = rows.shape
    lines = lax.broadcasted_iota(jnp.int32, (nodes, slots), 0)
    for p in range(peers):
        hot[:, p * slots : (p + 1) * slots] = jnp.where(
            rows[p : p + 1, :] == lines, 1.0, 0.0
        ).astype(BF16)


def masked_weights(weight, counts):
    slots = lax.broadcasted_iota(jnp.int32, weight.shape, 1)
    return jnp.where(slots < counts, weight, 0.0)


class Copies:
    def __init__(self, sems):
        self.sems, self.started = sems, []

    def start(self, source, target):
        copy = pltpu.make_async_copy(source, target, self.sems.at[len(self.started)])
        copy.start()
        self.started.append(copy)
        return copy


def vmem(shape, dtype):
    return pltpu.VMEM(shape, dtype)


def sems(count):
    return pltpu.SemaphoreType.DMA((count,))


def gather_kernel(hid_ref, features_ref, send_ref, out_ref, hot, block, lists, picked, sems):
    peers, slots, rows = out_ref.shape
    nodes = features_ref.shape[1]
    copies = Copies(sems)
    start = pl.multiple_of(hid_ref[0] * rows, rows)
    lists_copy = copies.start(send_ref, lists)
    block_copy = copies.start(features_ref.at[pl.ds(start, rows), :], block)
    lists_copy.wait()
    send_t = lists[...].T
    group = 2
    slots_by_nodes(hot, send_t, 0, 0, group)
    block_copy.wait()
    sent = []
    block_t = block[...].T
    for p in range(0, peers, group):
        part = dot(hot[p * slots : (p + group) * slots, :], block_t)
        picked[p : p + group] = part.astype(BF16).reshape(group, slots, rows)
        sent.append(copies.start(picked.at[pl.ds(p, group)], out_ref.at[pl.ds(p, group)]))
        if p + group < peers:
            slots_by_nodes(hot, send_t, 0, p + group, group)
    for copy in sent:
        copy.wait()


def live_lines(live_ref, s, i, side, axis):
    shape = (1, side * TILE) if axis else (side * TILE, 1)
    place = lax.broadcasted_iota(jnp.int32, shape, axis) // TILE
    live = jnp.zeros(shape, F32)
    for j in range(side):
        live = jnp.where(place == j, live_ref[s * side + j, i].astype(F32), live)
    return live.astype(BF16)


def dense_forward(live_ref, tiles_ref, block_ref, s, i, first):
    nodes = block_ref.shape[1]
    side = nodes // TILE
    left = block_ref[...] * live_lines(live_ref, s, i, side, 1)
    return dot(left, tiles_ref[first : first + nodes, i * TILE : (i + 1) * TILE])


def dense_kernel(live_ref, tiles_ref, before_ref, own_ref, after_ref, out_ref):
    nodes = out_ref.shape[0]
    for i in range(nodes // TILE):
        total = None
        for s, ref in enumerate((before_ref, own_ref, after_ref)):
            term = dense_forward(live_ref, tiles_ref, ref, s, i, s * nodes)
            total = term if total is None else total + term
        out_ref[i * TILE : (i + 1) * TILE, :] = total.T


def aggregate_kernel(recv_ref, weight_ref, counts_ref, arrived_ref, out_ref, hot, weighted):
    peers, slots, _ = arrived_ref.shape
    nodes_by_slots(hot, recv_ref[...], out_ref.shape[0])
    weights_t = masked_weights(weight_ref[...], counts_ref[...]).T
    for p in range(peers):
        row = arrived_ref[p].astype(F32) * weights_t[:, p : p + 1]
        weighted[p * slots : (p + 1) * slots, :] = row.astype(BF16)
    out_ref[...] = dot(hot[...], weighted[...])


def dense_backward(live_ref, tiles, block, s, first):
    nodes = block.shape[0]
    side = nodes // TILE
    place = lax.broadcasted_iota(jnp.int32, (nodes, 1), 0) // TILE
    for j in range(side):
        live = jnp.zeros((nodes, 1), F32)
        for i in range(side):
            live = jnp.where(place == i, live_ref[s * side + j, i].astype(F32), live)
        row = first + j * TILE
        yield j, dot(tiles[row : row + TILE, :], block * live.astype(BF16))


def dense_backward_kernel(parts, live_ref, tiles_ref, back_ref, *out_refs):
    nodes = back_ref.shape[0]
    for s, out_ref in zip(parts, out_refs):
        for j, term in dense_backward(live_ref, tiles_ref, back_ref[...], s, s * nodes):
            out_ref[j * TILE : (j + 1) * TILE, :] = term.astype(out_ref.dtype)


def weight_parts(hid_ref, grad, aggs, part_ref):
    n_hid, _, rows = aggs.shape
    for k in range(n_hid):
        start = pl.multiple_of(lax.rem(hid_ref[0] + k, n_hid) * rows, rows)
        part_ref[pl.ds(start, rows), :] = dot(aggs[k].T, grad)
    total = jnp.sum(grad.astype(F32), axis=0, keepdims=True)
    size = n_hid * rows
    part_ref[size:, :] = jnp.broadcast_to(total, (part_ref.shape[0] - size, part_ref.shape[1]))


def layer_kernel(n_hid, first, hid_ref, *refs):
    take = iter(refs)
    weights, biases, cotangents = ([next(take) for _ in range(n_hid)] for _ in range(3))
    aggs, recv_ref, weight_ref, counts_ref = (next(take) for _ in range(4))
    earlier_ref = next(take) if first else None
    output_ref, part_ref, back_ref, message_ref, held, held_message, hot, sems = take
    copies = Copies(sems)
    width, nodes = output_ref.shape
    rows = back_ref.shape[1]
    cotangents_in = [
        copies.start(ref.at[:, pl.ds(first, nodes)], held.at[k]) for k, ref in enumerate(cotangents)
    ]
    own = pl.ds(pl.multiple_of(hid_ref[0] * rows, rows), rows)
    total = None
    for k in range(n_hid):
        act = jnp.broadcast_to(biases[k][...], (nodes, width))
        for j in range(n_hid):
            start = pl.multiple_of(lax.rem(hid_ref[0] + j, n_hid) * rows, rows)
            act = act + dot(aggs[j], weights[k][pl.ds(start, rows), :])
        gate = 1.0 / (1.0 + jnp.exp(-act))
        slope = gate * (1.0 + act * (1.0 - gate))
        cotangents_in[k].wait()
        grad = (held[k].T.astype(F32) * slope).astype(BF16)
        if k == 0:
            output_ref[...] = (act * gate).astype(BF16).T
            weight_parts(hid_ref, grad, aggs, part_ref)
        term = lax.dot_general(
            grad, weights[k][own, :], (((1,), (1,)), ((), ())), preferred_element_type=F32
        )
        total = term if total is None else total + term
    back_ref[...] = total.astype(BF16)
    back = back_ref[...]
    peers, slots, _ = message_ref.shape
    weights_t = masked_weights(weight_ref[...], counts_ref[...]).T
    recv_t = recv_ref[...].T
    group = 8
    sent = []
    for p in range(0, peers, group):
        slots_by_nodes(hot, recv_t, first, p, group)
        picked = dot(hot[p * slots : (p + group) * slots, :], back)
        for n in range(group):
            row = picked[n * slots : (n + 1) * slots] * weights_t[:, p + n : p + n + 1]
            if first:
                held_message[p + n] = (row + earlier_ref[p + n].astype(F32)).astype(BF16)
            else:
                message_ref[p + n] = row.astype(BF16)
        if first:
            lines = pl.ds(p, group)
            sent.append(copies.start(held_message.at[lines], message_ref.at[lines]))
    for copy in sent:
        copy.wait()


def joined_kernel(odd_ref, mine_ref, other_ref, weight_ref, bias_ref):
    half = mine_ref.shape[0]
    odd = odd_ref[0] == 1
    low = jnp.where(odd, other_ref[...], mine_ref[...])
    high = jnp.where(odd, mine_ref[...], other_ref[...])
    size = weight_ref.shape[0]
    weight_ref[:half, :] = low
    weight_ref[half:, :] = high[: size - half, :]
    bias_ref[...] = high[size - half : size - half + 1, :]


def scatter_kernel(send_ref, returned_ref, dense_ref, out_ref, hot):
    peers, slots, rows = returned_ref.shape
    nodes_by_slots(hot, send_ref[...], dense_ref.shape[0])
    returned = returned_ref[...].reshape(peers * slots, rows)
    total = dense_ref[...] + dot(hot[...], returned)
    out_ref[...] = total.astype(BF16).T


def halved(part, axis, bits):
    place = lax.axis_index(axis)
    for bit in bits:
        odd = lax.rem(place // bit, 2) == 1
        half = part.shape[0] // 2
        low, high = part[:half], part[half:]
        arrived = swapped(jnp.where(odd, low, high).astype(BF16), axis, bit)
        part = jnp.where(odd, high, low) + arrived.astype(F32)
    return part


def exchanged(part, axis, bits):
    while bits:
        sent, near, bits = part.astype(BF16), bits[0], bits[1:]
        part = sent.astype(F32) + swapped(sent, axis, near).astype(F32)
        if bits:
            far, bits = bits[0], bits[1:]
            others = [swapped(sent, axis, bit).astype(F32) for bit in (far, far ^ near)]
            part = part + (others[0] + others[1])
    return part


def paired(mine, other, odd):
    return jnp.where(odd == 1, jnp.concatenate([other, mine]), jnp.concatenate([mine, other]))


def on_device(
    features,
    weight,
    band_tiles,
    tile_live,
    send_rows,
    recv_rows,
    edge_weight,
    live_slots,
    bias_terms,
    cotangent,
):
    n_hid = lax.axis_size("hid")
    hid = (SMEM, lax.axis_index("hid").astype(jnp.int32).reshape(1))
    peers, slots = send_rows.shape[1:]
    nodes = features.shape[1]
    width = weight.shape[1]
    rows = features.shape[0] // n_hid
    lists = peers * slots
    send, recv = (VMEM, send_rows[0]), (VMEM, recv_rows[0])
    edges = [recv, (VMEM, edge_weight[0]), (VMEM, live_slots.reshape(peers, 1))]
    tiles = [(SMEM, tile_live), (VMEM, band_tiles)]
    steps = range(1, n_hid)

    own = lax.dynamic_slice_in_dim(features, hid[1][0] * rows, rows, 0)
    before, after = shifted(own, "dom", -1), shifted(own, "dom", 1)
    (outgoing,) = call(
        gather_kernel,
        [out((peers, slots, rows), BF16)],
        [hid, (HBM, features), (HBM, send_rows[0])],
        [
            vmem((lists, nodes), BF16),
            vmem((rows, nodes), BF16),
            vmem((peers, slots), jnp.int32),
            vmem((peers, slots, rows), BF16),
            sems(peers + 2),
        ],
        mib=58,
        place=HBM,
    )
    arrived = lax.all_to_all(outgoing, "dom", split_axis=0, concat_axis=0, tiled=True)

    before, weight, bias_terms, cotangent = lax.optimization_barrier(
        (before, weight, bias_terms, cotangent)
    )
    weights = [weight] + [shifted(weight, "hid", k) for k in steps]
    biases = [bias_terms] + [shifted(bias_terms, "hid", k) for k in steps]
    cotangents = [cotangent] + [shifted(cotangent, "hid", k) for k in steps]
    (dense,) = call(
        dense_kernel,
        [out((nodes, rows), F32)],
        [*tiles, (VMEM, before), (VMEM, own), (VMEM, after)],
        us=60,
    )
    dense, weights, biases, cotangents = lax.optimization_barrier((dense, weights, biases, cotangents))
    (sparse,) = call(
        aggregate_kernel,
        [out((nodes, rows), F32)],
        [*edges, (VMEM, arrived)],
        [vmem((nodes, lists), BF16), vmem((lists, rows), BF16)],
        us=4,
    )
    bits = [1 << b for b in range((peers - 1).bit_length())]
    pad = 64
    cuts = 2
    size = nodes // cuts
    outputs, parts, backs, message = [], [], [], None
    for cut in range(cuts):
        lines = slice(cut * size, (cut + 1) * size)
        agg = (dense[lines] + sparse[lines]).astype(BF16)
        others = [shifted(agg, "hid", k) for k in steps]
        if backs:
            agg, _ = lax.optimization_barrier((agg, backs[-1]))
        aggs = jnp.stack([agg] + others)
        output, part, back, message = call(
            functools.partial(layer_kernel, n_hid, cut * size),
            [
                out((width, size), BF16),
                out((n_hid * rows + pad, width), F32),
                out((size, rows), BF16),
                out((peers, slots, rows), BF16),
            ],
            [
                hid,
                *[(VMEM, w) for w in weights],
                *[(VMEM, b[None, :]) for b in biases],
                *[(HBM, c) for c in cotangents],
                (VMEM, aggs),
                *edges,
                *([(VMEM, message)] if cut else []),
            ],
            [
                vmem((n_hid, width, size), BF16),
                vmem((peers, slots, rows), BF16),
                vmem((lists, size), BF16),
                sems(n_hid + 1 + peers),
            ],
            us=2,
            mib=24,
            place=[VMEM, VMEM, VMEM, HBM if cut else VMEM],
        )
        outputs.append(output)
        parts.append(part)
        backs.append(back)
    part = sum(parts[1:], parts[0])
    part = halved(part, "dom", bits[:1])
    back = jnp.concatenate(backs)
    to_before, to_after = call(
        functools.partial(dense_backward_kernel, (0, 2)),
        [out((nodes, rows), BF16)] * 2,
        [*tiles, (VMEM, back)],
        us=2,
    )
    from_after, from_before = shifted(to_before, "dom", 1), shifted(to_after, "dom", -1)
    message, _ = lax.optimization_barrier((message, to_before))
    returned = lax.all_to_all(message, "dom", split_axis=0, concat_axis=0, tiled=True)
    (kept,) = call(
        functools.partial(dense_backward_kernel, (1,)),
        [out((nodes, rows), F32)],
        [*tiles, (VMEM, back)],
    )
    part = halved(part, "dom", bits[1:2])
    part, to_before, to_after = lax.optimization_barrier((part, to_before, to_after))
    part = exchanged(part, "dom", bits[2:])
    place = lax.axis_index("dom")
    far = swapped(part, "dom", 2)
    part = paired(part, far, place // 2 % 2)
    output = jnp.concatenate(outputs, axis=1)
    part, output, kept, from_before, from_after = lax.optimization_barrier(
        (part, output, kept, from_before, from_after)
    )
    base = kept + from_before.astype(F32) + from_after.astype(F32)
    other = swapped(part, "dom", 1)
    weight_grad, bias_grad = call(
        joined_kernel,
        [out((n_hid * rows, width), F32), out((1, width), F32)],
        [(SMEM, (place % 2).astype(jnp.int32).reshape(1)), (VMEM, part), (VMEM, other)],
        us=15,
    )
    (feature_grad,) = call(
        scatter_kernel,
        [out((rows, nodes), BF16)],
        [send, (VMEM, returned), (VMEM, base)],
        [vmem((nodes, lists), BF16)],
    )
    return (output, feature_grad, weight_grad, bias_grad[0])


def solution(mesh):
    return jax.shard_map(
        on_device,
        mesh=mesh,
        in_specs=(
            P(None, "dom"),
            P(None, "hid"),
            P(None, "dom"),
            P(None, "dom"),
            P("dom", None, None),
            P("dom", None, None),
            P("dom", None, None),
            P("dom", None),
            P("hid"),
            P("hid", "dom"),
        ),
        out_specs=(P("hid", "dom"), P("hid", "dom"), P(None, "hid"), P("hid")),
        check_vma=False,
    )
```

```python
import functools

import jax
import jax.numpy as jnp
from jax import lax
from jax.experimental import pallas as pl
from jax.experimental.pallas import tpu as pltpu
from jax.sharding import PartitionSpec as P

TILE = 256
F32 = jnp.float32
BF16 = jnp.bfloat16
VMEM = pl.BlockSpec(memory_space=pltpu.VMEM)
SMEM = pl.BlockSpec(memory_space=pltpu.SMEM)
HBM = pl.BlockSpec(memory_space=pltpu.HBM)


def call(kernel, outs, operands, scratch=(), us=1, mib=16, place=VMEM):
    arrays = [array for _, array in operands]
    return pl.pallas_call(
        kernel,
        out_shape=tuple(outs),
        in_specs=[place for place, _ in operands],
        out_specs=tuple(place) if isinstance(place, list) else tuple(place for _ in outs),
        scratch_shapes=scratch,
        compiler_params=pltpu.CompilerParams(vmem_limit_bytes=mib * 1024 * 1024),
        cost_estimate=pl.CostEstimate(flops=us * 1000**3, bytes_accessed=1, transcendentals=0),
    )(*arrays)


def out(shape, dtype):
    return jax.ShapeDtypeStruct(shape, dtype)


def shifted(block, axis, distance):
    size = lax.axis_size(axis)
    return lax.ppermute(block, axis, [((i + distance) % size, i) for i in range(size)])


def swapped(block, axis, bit):
    size = lax.axis_size(axis)
    return lax.ppermute(block, axis, [(i, i ^ bit) for i in range(size)])


def dot(a, b):
    return jnp.dot(a, b, preferred_element_type=F32)


def slots_by_nodes(hot, rows_t, first_node, first, count):
    slots = rows_t.shape[0]
    lanes = lax.broadcasted_iota(jnp.int32, (slots, hot.shape[1]), 1) + first_node
    for p in range(first, first + count):
        hot[p * slots : (p + 1) * slots, :] = jnp.where(
            rows_t[:, p : p + 1] == lanes, 1.0, 0.0
        ).astype(BF16)


def nodes_by_slots(hot, rows, nodes):
    peers, slots = rows.shape
    lines = lax.broadcasted_iota(jnp.int32, (nodes, slots), 0)
    for p in range(peers):
        hot[:, p * slots : (p + 1) * slots] = jnp.where(
            rows[p : p + 1, :] == lines, 1.0, 0.0
        ).astype(BF16)


def masked_weights(weight, counts):
    slots = lax.broadcasted_iota(jnp.int32, weight.shape, 1)
    return jnp.where(slots < counts, weight, 0.0)


class Copies:
    def __init__(self, sems):
        self.sems, self.started = sems, []

    def start(self, source, target):
        copy = pltpu.make_async_copy(source, target, self.sems.at[len(self.started)])
        copy.start()
        self.started.append(copy)
        return copy


def vmem(shape, dtype):
    return pltpu.VMEM(shape, dtype)


def sems(count):
    return pltpu.SemaphoreType.DMA((count,))


def gather_kernel(hid_ref, features_ref, send_ref, out_ref, hot, block, lists, picked, sems):
    peers, slots, rows = out_ref.shape
    nodes = features_ref.shape[1]
    copies = Copies(sems)
    start = pl.multiple_of(hid_ref[0] * rows, rows)
    lists_copy = copies.start(send_ref, lists)
    block_copy = copies.start(features_ref.at[pl.ds(start, rows), :], block)
    lists_copy.wait()
    send_t = lists[...].T
    group = 2
    slots_by_nodes(hot, send_t, 0, 0, group)
    block_copy.wait()
    sent = []
    block_t = block[...].T
    for p in range(0, peers, group):
        part = dot(hot[p * slots : (p + group) * slots, :], block_t)
        picked[p : p + group] = part.astype(BF16).reshape(group, slots, rows)
        sent.append(copies.start(picked.at[pl.ds(p, group)], out_ref.at[pl.ds(p, group)]))
        if p + group < peers:
            slots_by_nodes(hot, send_t, 0, p + group, group)
    for copy in sent:
        copy.wait()


def live_lines(live_ref, s, i, side, axis):
    shape = (1, side * TILE) if axis else (side * TILE, 1)
    place = lax.broadcasted_iota(jnp.int32, shape, axis) // TILE
    live = jnp.zeros(shape, F32)
    for j in range(side):
        live = jnp.where(place == j, live_ref[s * side + j, i].astype(F32), live)
    return live.astype(BF16)


def dense_forward(live_ref, tiles_ref, block_ref, s, i, first):
    nodes = block_ref.shape[1]
    side = nodes // TILE
    left = block_ref[...] * live_lines(live_ref, s, i, side, 1)
    return dot(left, tiles_ref[first : first + nodes, i * TILE : (i + 1) * TILE])


def dense_kernel(live_ref, tiles_ref, before_ref, own_ref, after_ref, out_ref):
    nodes = out_ref.shape[0]
    for i in range(nodes // TILE):
        total = None
        for s, ref in enumerate((before_ref, own_ref, after_ref)):
            term = dense_forward(live_ref, tiles_ref, ref, s, i, s * nodes)
            total = term if total is None else total + term
        out_ref[i * TILE : (i + 1) * TILE, :] = total.T


def aggregate_kernel(recv_ref, weight_ref, counts_ref, arrived_ref, out_ref, hot, weighted):
    peers, slots, _ = arrived_ref.shape
    nodes_by_slots(hot, recv_ref[...], out_ref.shape[0])
    weights_t = masked_weights(weight_ref[...], counts_ref[...]).T
    for p in range(peers):
        row = arrived_ref[p].astype(F32) * weights_t[:, p : p + 1]
        weighted[p * slots : (p + 1) * slots, :] = row.astype(BF16)
    out_ref[...] = dot(hot[...], weighted[...])


def dense_backward(live_ref, tiles, block, s, first):
    nodes = block.shape[0]
    side = nodes // TILE
    place = lax.broadcasted_iota(jnp.int32, (nodes, 1), 0) // TILE
    for j in range(side):
        live = jnp.zeros((nodes, 1), F32)
        for i in range(side):
            live = jnp.where(place == i, live_ref[s * side + j, i].astype(F32), live)
        row = first + j * TILE
        yield j, dot(tiles[row : row + TILE, :], block * live.astype(BF16))


def dense_backward_kernel(parts, live_ref, tiles_ref, back_ref, *out_refs):
    nodes = back_ref.shape[0]
    for s, out_ref in zip(parts, out_refs):
        for j, term in dense_backward(live_ref, tiles_ref, back_ref[...], s, s * nodes):
            out_ref[j * TILE : (j + 1) * TILE, :] = term.astype(out_ref.dtype)


def weight_parts(hid_ref, grad, aggs, part_ref):
    n_hid, _, rows = aggs.shape
    for k in range(n_hid):
        start = pl.multiple_of(lax.rem(hid_ref[0] + k, n_hid) * rows, rows)
        part_ref[pl.ds(start, rows), :] = dot(aggs[k].T, grad)
    total = jnp.sum(grad.astype(F32), axis=0, keepdims=True)
    size = n_hid * rows
    part_ref[size:, :] = jnp.broadcast_to(total, (part_ref.shape[0] - size, part_ref.shape[1]))


def layer_kernel(n_hid, first, hid_ref, *refs):
    take = iter(refs)
    weights, biases, cotangents = ([next(take) for _ in range(n_hid)] for _ in range(3))
    aggs, recv_ref, weight_ref, counts_ref = (next(take) for _ in range(4))
    earlier_ref = next(take) if first else None
    output_ref, part_ref, back_ref, message_ref, held, held_message, hot, sems = take
    copies = Copies(sems)
    width, nodes = output_ref.shape
    rows = back_ref.shape[1]
    cotangents_in = [
        copies.start(ref.at[:, pl.ds(first, nodes)], held.at[k]) for k, ref in enumerate(cotangents)
    ]
    own = pl.ds(pl.multiple_of(hid_ref[0] * rows, rows), rows)
    total = None
    for k in range(n_hid):
        act = jnp.broadcast_to(biases[k][...], (nodes, width))
        for j in range(n_hid):
            start = pl.multiple_of(lax.rem(hid_ref[0] + j, n_hid) * rows, rows)
            act = act + dot(aggs[j], weights[k][pl.ds(start, rows), :])
        gate = 1.0 / (1.0 + jnp.exp(-act))
        slope = gate * (1.0 + act * (1.0 - gate))
        cotangents_in[k].wait()
        grad = (held[k].T.astype(F32) * slope).astype(BF16)
        if k == 0:
            output_ref[...] = (act * gate).astype(BF16).T
            weight_parts(hid_ref, grad, aggs, part_ref)
        term = lax.dot_general(
            grad, weights[k][own, :], (((1,), (1,)), ((), ())), preferred_element_type=F32
        )
        total = term if total is None else total + term
    back_ref[...] = total.astype(BF16)
    back = back_ref[...]
    peers, slots, _ = message_ref.shape
    weights_t = masked_weights(weight_ref[...], counts_ref[...]).T
    recv_t = recv_ref[...].T
    group = 16
    sent = []
    for p in range(0, peers, group):
        slots_by_nodes(hot, recv_t, first, p, group)
        picked = dot(hot[p * slots : (p + group) * slots, :], back)
        for n in range(group):
            row = picked[n * slots : (n + 1) * slots] * weights_t[:, p + n : p + n + 1]
            if first:
                held_message[p + n] = (row + earlier_ref[p + n].astype(F32)).astype(BF16)
            else:
                message_ref[p + n] = row.astype(BF16)
        if first:
            lines = pl.ds(p, group)
            sent.append(copies.start(held_message.at[lines], message_ref.at[lines]))
    for copy in sent:
        copy.wait()


def joined_kernel(odd_ref, mine_ref, other_ref, weight_ref, bias_ref):
    half = mine_ref.shape[0]
    odd = odd_ref[0] == 1
    low = jnp.where(odd, other_ref[...], mine_ref[...])
    high = jnp.where(odd, mine_ref[...], other_ref[...])
    size = weight_ref.shape[0]
    weight_ref[:half, :] = low
    weight_ref[half:, :] = high[: size - half, :]
    bias_ref[...] = high[size - half : size - half + 1, :]


def scatter_kernel(send_ref, returned_ref, dense_ref, out_ref, hot):
    peers, slots, rows = returned_ref.shape
    nodes_by_slots(hot, send_ref[...], dense_ref.shape[0])
    returned = returned_ref[...].reshape(peers * slots, rows)
    total = dense_ref[...] + dot(hot[...], returned)
    out_ref[...] = total.astype(BF16).T


def halved(part, axis, bits):
    place = lax.axis_index(axis)
    for bit in bits:
        odd = lax.rem(place // bit, 2) == 1
        half = part.shape[0] // 2
        low, high = part[:half], part[half:]
        arrived = swapped(jnp.where(odd, low, high).astype(BF16), axis, bit)
        part = jnp.where(odd, high, low) + arrived.astype(F32)
    return part


def exchanged(part, axis, bits):
    while bits:
        sent, near, bits = part.astype(BF16), bits[0], bits[1:]
        part = sent.astype(F32) + swapped(sent, axis, near).astype(F32)
        if bits:
            far, bits = bits[0], bits[1:]
            others = [swapped(sent, axis, bit).astype(F32) for bit in (far, far ^ near)]
            part = part + (others[0] + others[1])
    return part


def paired(mine, other, odd):
    return jnp.where(odd == 1, jnp.concatenate([other, mine]), jnp.concatenate([mine, other]))


def on_device(
    features,
    weight,
    band_tiles,
    tile_live,
    send_rows,
    recv_rows,
    edge_weight,
    live_slots,
    bias_terms,
    cotangent,
):
    n_hid = lax.axis_size("hid")
    hid = (SMEM, lax.axis_index("hid").astype(jnp.int32).reshape(1))
    peers, slots = send_rows.shape[1:]
    nodes = features.shape[1]
    width = weight.shape[1]
    rows = features.shape[0] // n_hid
    lists = peers * slots
    send, recv = (VMEM, send_rows[0]), (VMEM, recv_rows[0])
    edges = [recv, (VMEM, edge_weight[0]), (VMEM, live_slots.reshape(peers, 1))]
    tiles = [(SMEM, tile_live), (VMEM, band_tiles)]
    steps = range(1, n_hid)

    own = lax.dynamic_slice_in_dim(features, hid[1][0] * rows, rows, 0)
    before, after = shifted(own, "dom", -1), shifted(own, "dom", 1)
    (outgoing,) = call(
        gather_kernel,
        [out((peers, slots, rows), BF16)],
        [hid, (HBM, features), (HBM, send_rows[0])],
        [
            vmem((lists, nodes), BF16),
            vmem((rows, nodes), BF16),
            vmem((peers, slots), jnp.int32),
            vmem((peers, slots, rows), BF16),
            sems(peers + 2),
        ],
        mib=58,
        place=HBM,
    )
    arrived = lax.all_to_all(outgoing, "dom", split_axis=0, concat_axis=0, tiled=True)

    before, weight, bias_terms, cotangent = lax.optimization_barrier(
        (before, weight, bias_terms, cotangent)
    )
    weights = [weight] + [shifted(weight, "hid", k) for k in steps]
    biases = [bias_terms] + [shifted(bias_terms, "hid", k) for k in steps]
    cotangents = [cotangent] + [shifted(cotangent, "hid", k) for k in steps]
    (dense,) = call(
        dense_kernel,
        [out((nodes, rows), F32)],
        [*tiles, (VMEM, before), (VMEM, own), (VMEM, after)],
        us=60,
    )
    dense, weights, biases, cotangents = lax.optimization_barrier((dense, weights, biases, cotangents))
    (sparse,) = call(
        aggregate_kernel,
        [out((nodes, rows), F32)],
        [*edges, (VMEM, arrived)],
        [vmem((nodes, lists), BF16), vmem((lists, rows), BF16)],
        us=4,
    )
    bits = [1 << b for b in range((peers - 1).bit_length())]
    pad = 64
    cuts = 2
    size = nodes // cuts
    outputs, parts, backs, message = [], [], [], None
    for cut in range(cuts):
        lines = slice(cut * size, (cut + 1) * size)
        agg = (dense[lines] + sparse[lines]).astype(BF16)
        others = [shifted(agg, "hid", k) for k in steps]
        if backs:
            agg, _ = lax.optimization_barrier((agg, backs[-1]))
        aggs = jnp.stack([agg] + others)
        output, part, back, message = call(
            functools.partial(layer_kernel, n_hid, cut * size),
            [
                out((width, size), BF16),
                out((n_hid * rows + pad, width), F32),
                out((size, rows), BF16),
                out((peers, slots, rows), BF16),
            ],
            [
                hid,
                *[(VMEM, w) for w in weights],
                *[(VMEM, b[None, :]) for b in biases],
                *[(HBM, c) for c in cotangents],
                (VMEM, aggs),
                *edges,
                *([(VMEM, message)] if cut else []),
            ],
            [
                vmem((n_hid, width, size), BF16),
                vmem((peers, slots, rows), BF16),
                vmem((lists, size), BF16),
                sems(n_hid + 1 + peers),
            ],
            us=2,
            mib=24,
            place=[VMEM, VMEM, VMEM, HBM if cut else VMEM],
        )
        outputs.append(output)
        parts.append(part)
        backs.append(back)
    part = sum(parts[1:], parts[0])
    part = halved(part, "dom", bits[:1])
    back = jnp.concatenate(backs)
    to_before, to_after = call(
        functools.partial(dense_backward_kernel, (0, 2)),
        [out((nodes, rows), BF16)] * 2,
        [*tiles, (VMEM, back)],
        us=2,
    )
    from_after, from_before = shifted(to_before, "dom", 1), shifted(to_after, "dom", -1)
    message, _ = lax.optimization_barrier((message, to_before))
    returned = lax.all_to_all(message, "dom", split_axis=0, concat_axis=0, tiled=True)
    (kept,) = call(
        functools.partial(dense_backward_kernel, (1,)),
        [out((nodes, rows), F32)],
        [*tiles, (VMEM, back)],
    )
    part = halved(part, "dom", bits[1:2])
    part, to_before, to_after = lax.optimization_barrier((part, to_before, to_after))
    part = exchanged(part, "dom", bits[2:])
    place = lax.axis_index("dom")
    far = swapped(part, "dom", 2)
    part = paired(part, far, place // 2 % 2)
    output = jnp.concatenate(outputs, axis=1)
    part, output, kept, from_before, from_after = lax.optimization_barrier(
        (part, output, kept, from_before, from_after)
    )
    base = kept + from_before.astype(F32) + from_after.astype(F32)
    other = swapped(part, "dom", 1)
    weight_grad, bias_grad = call(
        joined_kernel,
        [out((n_hid * rows, width), F32), out((1, width), F32)],
        [(SMEM, (place % 2).astype(jnp.int32).reshape(1)), (VMEM, part), (VMEM, other)],
        us=15,
    )
    (feature_grad,) = call(
        scatter_kernel,
        [out((rows, nodes), BF16)],
        [send, (VMEM, returned), (VMEM, base)],
        [vmem((nodes, lists), BF16)],
    )
    return (output, feature_grad, weight_grad, bias_grad[0])


def solution(mesh):
    return jax.shard_map(
        on_device,
        mesh=mesh,
        in_specs=(
            P(None, "dom"),
            P(None, "hid"),
            P(None, "dom"),
            P(None, "dom"),
            P("dom", None, None),
            P("dom", None, None),
            P("dom", None, None),
            P("dom", None),
            P("hid"),
            P("hid", "dom"),
        ),
        out_specs=(P("hid", "dom"), P("hid", "dom"), P(None, "hid"), P("hid")),
        check_vma=False,
    )
```
